256 devices in a mesh: kblk: 64 (over y, z, core), amp: 4 (over x).
Axes of the slice: x: 4, y: 4, z: 8, core: 2. Of those that a mesh axis runs over, the one named last changes fastest.
Arguments:
- integrals: bfloat16 [32768, 16384], P(('kblk', 'amp')), may hold values from -0.046875 to 0.046875
- row_owner: int32 [32768, 1], P(('kblk', 'amp')), may hold values from 0 to 63; in each aligned block of 128 rows (0 to 127, 128 to 255, ...) at most 4 rows name the same one
- lambda_amps: bfloat16 [64, 512, 16384], P('kblk', 'amp'), may hold values from -6 to 6
Outputs:
- ladder: float32 [32768, 512], P(('kblk', 'amp'))
The draws below stay inside these ranges and needn't reach their ends.
Inputs may be any that keep to these rules, and one draw needn't show every extreme that they name: Among the 128 rows of one device (aligned blocks of row_owner), at most 4 name the same k-triple, and some k-triple is named by exactly 4 of them.
All inputs are finite; a program needn't handle non-finite values.
Results may differ from the reference program's by a relative error of at most 0.0003.
Values may be sent and summed in bfloat16 or wider, within the bound.
No kernel may reach another device: no remote copies, remote signals or barrier semaphores. Data moves between devices by JAX's collectives and lax.ppermute only.
A program may use at most 128 MiB of HBM per device.

```python
import math
import jax
import jax.numpy as jnp
import numpy as np
from jax import lax

VV = 16384
NPAIR = 512
ROWS_DEV = 128
CAP = 4
TRIPLES = 64
ROWS = 32768
N_KBLK = 64
N_AMP = 4


def steps_of(key, extent, split, low, high):
    def one(dim, parts):
        draws = jax.random.uniform(jax.random.fold_in(jax.random.fold_in(key, 6), dim), (parts,), jnp.float32, low / len(split), high / len(split))
        return jnp.repeat(jnp.exp(draws), extent[dim] // parts).reshape((-1,) + (1,) * (len(extent) - dim - 1))

    gain = one(*split[0])
    for cut in split[1:]:
        gain = gain * one(*cut)
    return gain


def routed_block(own_key, own, number, rows, amount, top, most, slope):
    sequence = jax.random.permutation(own_key, amount)
    crowded, usual = portions_of(amount, rows * top, most, slope, True), portions_of(amount, rows * top, most, slope, False)
    places = jnp.arange(amount)

    def named(lengths, rotation):
        used = int((lengths > 0).sum())
        fixed = max(1, used // 4)
        shifted = fixed + (places - fixed + rotation * (used - fixed)) % max(1, amount - fixed)
        return jnp.zeros((amount,), jnp.int32).at[sequence[jnp.where(places < fixed, places, shifted)]].set(jnp.asarray(lengths, jnp.int32))

    lengths = jnp.where(number % 4 == 0, named(crowded, number // 4), named(usual, number - number // 4 - 1))
    mixed = jax.random.permutation(jax.random.fold_in(own, 3), amount)
    source_of, taker = mixed[0:amount // 2 * 2:2], mixed[1:amount // 2 * 2:2]
    margin = jnp.minimum(lengths[source_of] - 1, most - lengths[taker]) // 2
    margin = jnp.where((source_of == sequence[0]) | (taker == sequence[0]) | (lengths[taker] == 0), 0, jnp.maximum(margin, 0))
    shifted = jax.random.randint(jax.random.fold_in(own, 4), (amount // 2,), 0, 1 << 20) % (margin + 1)
    lengths = lengths.at[source_of].add(-shifted).at[taker].add(shifted)
    labels = jnp.searchsorted(jnp.cumsum(lengths), jnp.arange(rows * top), side="right").astype(jnp.int32)
    listing = labels.reshape(top, rows).T
    listing = listing[jax.random.permutation(jax.random.fold_in(own, 1), rows)]
    rotation = jax.random.randint(jax.random.fold_in(own, 2), (rows, 1), 0, top)
    return jnp.take_along_axis(listing, (jnp.arange(top)[None, :] + rotation) % top, axis=1)


def portions_of(count, total, reach, lean, full):
    portions = [(1 << 20) // math.isqrt(standing ** lean) + 1 for standing in range(1, count + 1)]
    largest = reach if full else min(reach, max(-(-total // count), total * portions[0] // sum(portions)))
    least = 1 if total - largest >= count - 1 else 0
    given, spare = [largest] + [least] * (count - 1), total - largest - least * (count - 1)
    while spare > 0:
        free = [i for i in range(1, count) if given[i] < largest] or [i for i in range(1, count) if given[i] < reach]
        mass, budget = sum([portions[i] for i in free]), spare
        for i in free:
            addition = min(reach - given[i], max(1, budget * portions[i] // mass), spare)
            given[i] = given[i] + addition
            spare = spare - addition
    return np.array(given)


def bell_draw(stream_key, shape, width, most, cuts=(), held_as=jnp.bfloat16):
    array = jax.random.normal(stream_key, shape, jnp.float32) * width
    if len(cuts) > 0:
        array = steps_of(stream_key, shape, cuts, -0.22, 0.18) * array
    return jnp.clip(array, min=-most, max=most).astype(held_as)


def setup_inputs(seed: int = 0) -> dict:
    keys = jax.random.split(jax.random.key(seed), 4)
    integrals = bell_draw(keys[0], (ROWS, VV), VV ** -0.5, 0.046875, ((0, 256),))
    row_owner_keys = jax.random.split(jax.random.fold_in(keys[1], 1), ROWS // ROWS_DEV)
    row_owner_turns = jax.random.permutation(jax.random.fold_in(keys[1], 3), ROWS // ROWS_DEV)
    row_owner = jax.vmap(lambda own, number: routed_block(jax.random.fold_in(keys[1], 2), own, number, ROWS_DEV, N_KBLK, 1, CAP, 2))(row_owner_keys, row_owner_turns).reshape((ROWS, 1))
    lambda_amps = bell_draw(keys[2], (TRIPLES, NPAIR, VV), 1.0, 6.0, ((0, 64), (1, 4)))
    return {"integrals": integrals, "row_owner": row_owner, "lambda_amps": lambda_amps}


def reference(integrals, row_owner, lambda_amps):
    owner = row_owner[:, 0]
    limit = N_AMP * N_KBLK * CAP

    def accumulate(triple, total):
        member = owner == triple
        chosen = jnp.nonzero(member, size=limit, fill_value=0)[0].astype(jnp.int32)
        count = jnp.sum(member.astype(jnp.int32))
        valid = (jnp.arange(limit, dtype=jnp.int32) < count).astype(jnp.float32)
        amps = lax.dynamic_index_in_dim(lambda_amps, triple, 0, keepdims=False)
        values = jnp.dot(integrals[chosen], amps.T, preferred_element_type=jnp.float32)
        return total.at[chosen].add(values * valid[:, None])

    start = jnp.zeros((integrals.shape[0], lambda_amps.shape[1]), jnp.float32)
    return lax.fori_loop(0, N_KBLK, accumulate, start)
```

```python
import jax
import jax.numpy as jnp
from jax import lax
from jax.experimental import pallas as pl
from jax.experimental.pallas import tpu as pltpu
from jax.sharding import PartitionSpec as P

CAP = 4
BLOCK = 2 * CAP
CHIPS = 32
VMEM = 48 * 1024 * 1024
SIBLING = [(k, k ^ 1) for k in range(2 * CHIPS)]
SAME_CORE = [[2 * chip + core for chip in range(CHIPS)] for core in range(2)]


def place_kernel(line_ref, mine_ref, theirs_ref, out_ref):
    lines = out_ref.shape[0]
    number = lax.broadcasted_iota(jnp.int32, (lines, line_ref.shape[1]), 0)
    pick = (number == line_ref[...]).astype(jnp.bfloat16)
    both = jnp.concatenate([mine_ref[...], theirs_ref[...]], axis=0)
    out_ref[...] = jnp.dot(pick, both, preferred_element_type=jnp.float32).astype(jnp.bfloat16)


def place(line, mine, theirs):
    rows, cols = mine.shape
    lines, block = CHIPS * BLOCK, min(2048, cols)
    return pl.pallas_call(
        place_kernel,
        grid=(cols // block,),
        in_specs=[
            pl.BlockSpec((1, 2 * rows), lambda i: (0, 0)),
            pl.BlockSpec((rows, block), lambda i: (0, i)),
            pl.BlockSpec((rows, block), lambda i: (0, i)),
        ],
        out_specs=pl.BlockSpec((lines, block), lambda i: (0, i)),
        out_shape=jax.ShapeDtypeStruct((lines, cols), jnp.bfloat16),
        compiler_params=pltpu.CompilerParams(vmem_limit_bytes=VMEM),
        cost_estimate=pl.CostEstimate(
            flops=4 * lines * rows * cols,
            bytes_accessed=2 * (2 * rows + lines) * cols,
            transcendentals=0,
        ),
        name="place",
    )(line, mine, theirs)


def multiply_kernel(rows_ref, amps_ref, out_ref):
    @pl.when(pl.program_id(0) == 0)
    def _():
        out_ref[...] = jnp.zeros_like(out_ref)

    out_ref[...] += lax.dot_general(
        rows_ref[...], amps_ref[...], (((1,), (1,)), ((), ())), preferred_element_type=jnp.float32
    )


def multiply(rows, amps):
    lines, cols = rows.shape
    pairs, block = amps.shape[0], min(2048, cols)
    return pl.pallas_call(
        multiply_kernel,
        grid=(cols // block,),
        in_specs=[
            pl.BlockSpec((lines, block), lambda i: (0, i)),
            pl.BlockSpec((pairs, block), lambda i: (0, i)),
        ],
        out_specs=pl.BlockSpec((lines, pairs), lambda i: (0, 0)),
        out_shape=jax.ShapeDtypeStruct((lines, pairs), jnp.float32),
        compiler_params=pltpu.CompilerParams(vmem_limit_bytes=VMEM),
        cost_estimate=pl.CostEstimate(
            flops=2 * lines * pairs * cols,
            bytes_accessed=2 * (lines + pairs) * cols + 4 * lines * pairs,
            transcendentals=0,
        ),
        name="multiply",
    )(rows, amps)


def body(integrals, row_owner, lambda_amps):
    peers = lax.axis_size("kblk")
    core = lax.axis_index("kblk") % 2
    rows_here, cols = integrals.shape
    theirs = lax.ppermute(integrals, "kblk", SIBLING)

    owner = row_owner[:, 0]
    number = jnp.arange(rows_here, dtype=jnp.int32)
    earlier = (owner[:, None] == owner[None, :]) & (number[None, :] < number[:, None])
    slot = jnp.sum(earlier.astype(jnp.int32), axis=1)
    line = (owner // 2) * BLOCK + core * CAP + slot
    stays = owner % 2 == core
    sent = lax.ppermute(jnp.where(stays, -1, line)[None, :], "kblk", SIBLING)
    lines = jnp.concatenate([jnp.where(stays, line, -1)[None, :], sent], axis=1)

    whole_lambda = lax.all_gather(lambda_amps, "amp", axis=1, tiled=True)[0]
    pairs = whole_lambda.shape[0]

    placed = place(lines, integrals, theirs)
    arrived = lax.all_to_all(
        placed.reshape(CHIPS, BLOCK, cols),
        "kblk",
        split_axis=0,
        concat_axis=0,
        axis_index_groups=SAME_CORE,
        tiled=True,
    )
    values = multiply(arrived.reshape(CHIPS * BLOCK, cols), whole_lambda)
    returned = lax.all_to_all(
        values.reshape(peers, CAP, pairs), "kblk", split_axis=0, concat_axis=0, tiled=True
    )
    return returned.reshape(peers * CAP, pairs)[owner * CAP + slot]


def solution(mesh):
    placed = (P(("kblk", "amp"), None), P(("kblk", "amp"), None), P("kblk", "amp", None))
    return jax.shard_map(
        body, mesh=mesh, in_specs=placed, out_specs=P(("kblk", "amp"), None), check_vma=False
    )
```

```python
import jax
import jax.numpy as jnp
from jax import lax
from jax.experimental import pallas as pl
from jax.experimental.pallas import tpu as pltpu
from jax.sharding import PartitionSpec as P

CAP = 4
BLOCK = 2 * CAP
SHIFTS = (0, 1, 3, 2)
VMEM = 48 * 1024 * 1024


def place_kernel(owner_ref, low_ref, high_ref, out_ref, pick_ref):
    lines, rows = out_ref.shape[0], low_ref.shape[0]

    @pl.when(pl.program_id(0) == 0)
    def _():
        owner = owner_ref[...]
        across = jnp.broadcast_to(owner.astype(jnp.float32), (rows, rows))
        down = across.T
        first = lax.broadcasted_iota(jnp.int32, (rows, rows), 0)
        second = lax.broadcasted_iota(jnp.int32, (rows, rows), 1)
        earlier = jnp.where((across == down) & (first < second), 1, 0)
        line = owner * BLOCK + jnp.sum(earlier, axis=0, keepdims=True)
        number = lax.broadcasted_iota(jnp.int32, (lines, rows), 0)
        pick_ref[:, :rows] = jnp.where(number == line, 1.0, 0.0).astype(jnp.bfloat16)
        pick_ref[:, rows:] = jnp.where(number == line + CAP, 1.0, 0.0).astype(jnp.bfloat16)

    both = jnp.concatenate([low_ref[...], high_ref[...]], axis=0)
    out_ref[...] = jnp.dot(
        pick_ref[...], both, preferred_element_type=jnp.float32
    ).astype(jnp.bfloat16)


def place(owner, integrals, peers):
    rows, cols = integrals.shape
    lines, width = peers * BLOCK, cols // 2
    block = min(1024, width)
    steps = width // block
    return pl.pallas_call(
        place_kernel,
        grid=(steps,),
        in_specs=[
            pl.BlockSpec((1, rows), lambda i: (0, 0)),
            pl.BlockSpec((rows, block), lambda i: (0, i)),
            pl.BlockSpec((rows, block), lambda i: (0, steps + i)),
        ],
        out_specs=pl.BlockSpec((lines, block), lambda i: (0, i)),
        out_shape=jax.ShapeDtypeStruct((lines, width), jnp.bfloat16),
        scratch_shapes=[pltpu.VMEM((lines, 2 * rows), jnp.bfloat16)],
        compiler_params=pltpu.CompilerParams(vmem_limit_bytes=VMEM),
        cost_estimate=pl.CostEstimate(
            flops=4 * lines * rows * width,
            bytes_accessed=2 * (2 * rows + lines) * width,
            transcendentals=0,
        ),
        name="place",
    )(owner, integrals, integrals)


def multiply_kernel(amp_ref, rows_ref, *refs):
    amp_refs, out_ref, total_ref = refs[:-2], refs[-2], refs[-1]
    step, last = pl.program_id(0), pl.num_programs(0) - 1

    @pl.when(step == 0)
    def _():
        total_ref[...] = jnp.zeros_like(total_ref)

    rows = rows_ref[...]
    half = lax.broadcasted_iota(jnp.int32, rows.shape, 0) // CAP % 2
    zero = jnp.zeros_like(rows)
    wide = jnp.concatenate(
        [jnp.where(half == 0, rows, zero), jnp.where(half == 1, rows, zero)], axis=1
    )
    count = len(amp_refs) // 2
    low = jnp.concatenate([ref[...] for ref in amp_refs[:count]], axis=0)
    high = jnp.concatenate([ref[...] for ref in amp_refs[count:]], axis=0)
    amps = jnp.concatenate([low, high], axis=1)
    total_ref[...] += lax.dot_general(
        wide, amps, (((1,), (1,)), ((), ())), preferred_element_type=jnp.float32
    )

    @pl.when(step == last)
    def _():
        pairs = amp_refs[0].shape[0]
        for i, shift in enumerate(SHIFTS):
            at = (amp_ref[0] + len(SHIFTS) - shift) % len(SHIFTS)
            there = pl.ds(pl.multiple_of(at * pairs, pairs), pairs)
            here = slice(i * pairs, (i + 1) * pairs)
            for source in range(out_ref.shape[0]):
                start = source * BLOCK
                out_ref[source, :, there] = (
                    total_ref[start : start + CAP, here]
                    + total_ref[start + CAP : start + BLOCK, here]
                )


def multiply(amp, rows, shards, peers):
    lines, width = rows.shape
    pairs, block = shards[0].shape[0], min(1024, width)
    steps, count = width // block, len(shards)
    return pl.pallas_call(
        multiply_kernel,
        grid=(steps,),
        in_specs=[
            pl.BlockSpec(memory_space=pltpu.SMEM),
            pl.BlockSpec((lines, block), lambda i: (0, i)),
        ]
        + [pl.BlockSpec((pairs, block), lambda i: (0, i))] * count
        + [pl.BlockSpec((pairs, block), lambda i: (0, steps + i))] * count,
        out_specs=pl.BlockSpec((peers, CAP, count * pairs), lambda i: (0, 0, 0)),
        out_shape=jax.ShapeDtypeStruct((peers, CAP, count * pairs), jnp.float32),
        scratch_shapes=[pltpu.VMEM((lines, count * pairs), jnp.float32)],
        compiler_params=pltpu.CompilerParams(vmem_limit_bytes=VMEM),
        cost_estimate=pl.CostEstimate(
            flops=4 * lines * count * pairs * width,
            bytes_accessed=2 * (lines + 2 * count * pairs) * width,
            transcendentals=0,
        ),
        name="multiply",
    )(amp, rows, *shards, *shards)


def body(integrals, row_owner, lambda_amps):
    peers, amps = lax.axis_size("kblk"), lax.axis_size("amp")
    amp = lax.axis_index("amp").astype(jnp.int32)
    mine = lambda_amps[0]
    shards = [mine] + [
        lax.ppermute(mine, "amp", [(i, (i + shift) % amps) for i in range(amps)])
        for shift in SHIFTS[1:]
    ]

    rows_here = integrals.shape[0]
    owner = row_owner[:, 0]
    placed = place(owner[None, :], integrals, peers)
    width = placed.shape[1]
    arrived = lax.all_to_all(
        placed.reshape(peers, BLOCK, width), "kblk", split_axis=0, concat_axis=0, tiled=True
    )
    values = multiply(amp[None], arrived.reshape(peers * BLOCK, width), shards, peers)
    returned = lax.all_to_all(values, "kblk", split_axis=0, concat_axis=0, tiled=True)

    number = jnp.arange(rows_here, dtype=jnp.int32)
    earlier = (owner[:, None] == owner[None, :]) & (number[None, :] < number[:, None])
    slot = jnp.sum(earlier.astype(jnp.int32), axis=1)
    return returned.reshape(peers * CAP, values.shape[2])[owner * CAP + slot]


def solution(mesh):
    placed = (P(("kblk", "amp"), None), P(("kblk", "amp"), None), P("kblk", "amp", None))
    return jax.shard_map(
        body, mesh=mesh, in_specs=placed, out_specs=P(("kblk", "amp"), None), check_vma=False
    )
```

```python
import jax
import jax.numpy as jnp
from jax import lax
from jax.experimental import pallas as pl
from jax.experimental.pallas import tpu as pltpu
from jax.sharding import PartitionSpec as P

CAP = 4
BLOCK = 2 * CAP
PLACE_STEPS = 8
MULTIPLY_STEPS = 8


def whole_in(space):
    return pl.BlockSpec(memory_space=space)


def place_kernel(swap_ref, owner_ref, integrals_ref, out_ref, both_ref, placed_ref, pick_ref, sem):
    rows, (lines, width) = integrals_ref.shape[0], out_ref.shape
    block = width // PLACE_STEPS
    fetches = [
        [
            pltpu.make_async_copy(
                integrals_ref.at[:, pl.ds(half * width + i * block, block)],
                both_ref.at[pl.ds(half * rows, rows), pl.ds(i * block, block)],
                sem.at[i, half],
            )
            for half in range(2)
        ]
        for i in range(PLACE_STEPS)
    ]
    for pair in fetches:
        for copy in pair:
            copy.start()

    owner = owner_ref[...]
    across = jnp.broadcast_to(owner.astype(jnp.float32), (rows, rows))
    down = across.T
    first = lax.broadcasted_iota(jnp.int32, (rows, rows), 0)
    second = lax.broadcasted_iota(jnp.int32, (rows, rows), 1)
    earlier = jnp.where((across == down) & (first < second), 1, 0)
    line = owner * BLOCK + jnp.sum(earlier, axis=0, keepdims=True)
    number = lax.broadcasted_iota(jnp.int32, (lines, rows), 0)
    swap = swap_ref[0] * CAP
    pick_ref[:, :rows] = jnp.where(number == line + swap, 1.0, 0.0).astype(jnp.bfloat16)
    pick_ref[:, rows:] = jnp.where(number == line + (CAP - swap), 1.0, 0.0).astype(jnp.bfloat16)

    writes = []
    for i, pair in enumerate(fetches):
        for copy in pair:
            copy.wait()
        here = pl.ds(i * block, block)
        placed_ref[:, here] = jnp.dot(
            pick_ref[...], both_ref[:, here], preferred_element_type=jnp.float32
        ).astype(jnp.bfloat16)
        write = pltpu.make_async_copy(placed_ref.at[:, here], out_ref.at[:, here], sem.at[i, 2])
        write.start()
        writes.append(write)
    for write in writes:
        write.wait()


def place(swap, owner, integrals, peers):
    rows, cols = integrals.shape
    lines, width = peers * BLOCK, cols // 2
    return pl.pallas_call(
        place_kernel,
        in_specs=[whole_in(pltpu.SMEM), whole_in(pltpu.VMEM), whole_in(pl.ANY)],
        out_specs=whole_in(pl.ANY),
        out_shape=pltpu.HBM((lines, width), jnp.bfloat16),
        scratch_shapes=[
            pltpu.VMEM((2 * rows, width), jnp.bfloat16),
            pltpu.VMEM((lines, width), jnp.bfloat16),
            pltpu.VMEM((lines, 2 * rows), jnp.bfloat16),
            pltpu.SemaphoreType.DMA((PLACE_STEPS, 3)),
        ],
        compiler_params=pltpu.CompilerParams(vmem_limit_bytes=24 * 1024 * 1024),
        cost_estimate=pl.CostEstimate(
            flops=4 * lines * rows * width,
            bytes_accessed=2 * (2 * rows + lines) * width,
            transcendentals=0,
        ),
        name="place",
    )(swap, owner, pltpu.with_memory_space_constraint(integrals, pltpu.HBM))


def multiply_kernel(
    amp_ref, rows_ref, mine_ref, left_ref, right_ref, top_ref, bottom_ref,
    out_ref, near_ref, amps_ref, low_ref, high_ref, sem,
):
    lines, width = rows_ref.shape
    upper = lines // 2
    block = width // MULTIPLY_STEPS
    pairs = mine_ref.shape[0]
    count = amps_ref.shape[0] // pairs
    shards = (
        (mine_ref, 0, 0),
        (left_ref, 1, 0),
        (right_ref, 3, 0),
        (top_ref, 2, 0),
        (bottom_ref, 2, pairs // 2),
    )

    def fetches(i):
        here = pl.ds(pl.multiple_of(i * block, block), block)
        copies = [
            pltpu.make_async_copy(rows_ref.at[:, here], near_ref.at[:, here], sem.at[i, 0])
        ]
        for half in range(2):
            here = pl.ds(pl.multiple_of(half * width + i * block, block), block)
            for k, (ref, shift, skip) in enumerate(shards):
                at = (amp_ref[0] + count - shift) % count
                there = pl.ds(pl.multiple_of(at * pairs + skip, pairs // 2), ref.shape[0])
                copies.append(
                    pltpu.make_async_copy(
                        ref.at[:, here],
                        amps_ref.at[there, here],
                        sem.at[i, 1 + half * len(shards) + k],
                    )
                )
        return copies

    for i in range(MULTIPLY_STEPS):
        for copy in fetches(i):
            copy.start()
    group = lax.broadcasted_iota(jnp.int32, (upper, block), 0) // CAP % 2
    low_ref[...] = jnp.zeros_like(low_ref)
    high_ref[...] = jnp.zeros_like(high_ref)

    @pl.loop(0, MULTIPLY_STEPS)
    def _(i):
        for copy in fetches(i):
            copy.wait()
        here = pl.ds(pl.multiple_of(i * block, block), block)
        first, second = near_ref[:upper, here], near_ref[upper:, here]
        for half, total_ref in enumerate((low_ref, high_ref)):
            there = pl.ds(pl.multiple_of(half * width + i * block, block), block)
            total_ref[...] += lax.dot_general(
                jnp.where(group == half, first, second),
                amps_ref[:, there],
                (((1,), (1,)), ((), ())),
                preferred_element_type=jnp.float32,
            )

    half_peers = upper // BLOCK
    for source in range(half_peers):
        start = source * BLOCK
        top, bottom = slice(start, start + CAP), slice(start + CAP, start + BLOCK)
        out_ref[source] = low_ref[top, :] + high_ref[bottom, :]
        out_ref[half_peers + source] = low_ref[bottom, :] + high_ref[top, :]


def multiply(amp, rows, shards, peers, amps):
    lines, width = rows.shape
    pairs = amps * shards[0].shape[0]
    return pl.pallas_call(
        multiply_kernel,
        in_specs=[whole_in(pltpu.SMEM)] + [whole_in(pl.ANY)] * (1 + len(shards)),
        out_specs=whole_in(pltpu.VMEM),
        out_shape=jax.ShapeDtypeStruct((peers, CAP, pairs), jnp.float32),
        scratch_shapes=[
            pltpu.VMEM((lines, width), jnp.bfloat16),
            pltpu.VMEM((pairs, 2 * width), jnp.bfloat16),
            pltpu.VMEM((lines // 2, pairs), jnp.float32),
            pltpu.VMEM((lines // 2, pairs), jnp.float32),
            pltpu.SemaphoreType.DMA((MULTIPLY_STEPS, 1 + 2 * len(shards))),
        ],
        compiler_params=pltpu.CompilerParams(vmem_limit_bytes=36 * 1024 * 1024),
        cost_estimate=pl.CostEstimate(
            flops=2 * lines * pairs * width,
            bytes_accessed=2 * (lines + 2 * pairs) * width,
            transcendentals=0,
        ),
        name="multiply",
    )(amp, *[pltpu.with_memory_space_constraint(x, pltpu.HBM) for x in (rows, *shards)])


def body(integrals, row_owner, lambda_amps):
    peers, amps = lax.axis_size("kblk"), lax.axis_size("amp")
    amp = lax.axis_index("amp").astype(jnp.int32)
    swap = (lax.axis_index("kblk") >= peers // 2).astype(jnp.int32)
    mine = lambda_amps[0]
    middle = mine.shape[0] // 2
    ahead = [(i, (i + 1) % amps) for i in range(amps)]
    back = [(i, (i - 1) % amps) for i in range(amps)]
    left, right = lax.ppermute(mine, "amp", ahead), lax.ppermute(mine, "amp", back)
    top = lax.ppermute(left[:middle], "amp", ahead)
    bottom = lax.ppermute(right[middle:], "amp", back)
    shards = (mine, left, right, top, bottom)

    rows_here = integrals.shape[0]
    owner = row_owner[:, 0]
    placed = place(swap[None], owner[None, :], integrals, peers)
    width = placed.shape[1]
    arrived = lax.all_to_all(
        placed.reshape(peers, BLOCK, width), "kblk", split_axis=0, concat_axis=0, tiled=True
    )
    values = multiply(amp[None], arrived.reshape(peers * BLOCK, width), shards, peers, amps)
    returned = lax.all_to_all(values, "kblk", split_axis=0, concat_axis=0, tiled=True)

    number = jnp.arange(rows_here, dtype=jnp.int32)
    earlier = (owner[:, None] == owner[None, :]) & (number[None, :] < number[:, None])
    slot = jnp.sum(earlier.astype(jnp.int32), axis=1)
    return returned.reshape(peers * CAP, values.shape[2])[owner * CAP + slot]


def solution(mesh):
    placed = (P(("kblk", "amp"), None), P(("kblk", "amp"), None), P("kblk", "amp", None))
    return jax.shard_map(
        body, mesh=mesh, in_specs=placed, out_specs=P(("kblk", "amp"), None), check_vma=False
    )
```

```python
import jax
import jax.numpy as jnp
from jax import lax
from jax.experimental import pallas as pl
from jax.experimental.pallas import tpu as pltpu
from jax.sharding import PartitionSpec as P

CAP = 4
LARGEST = 32767.0
STEPS = 64
LANES = 128
BLOCK = 2 * CAP
PLACE_STEPS = 8
MULTIPLY_BLOCKS = (512, 512, 1024, 1024, 1024, 1024, 1024, 1024, 512, 512)


def whole_in(space):
    return pl.BlockSpec(memory_space=space)


def slots_of(owner):
    rows = owner.shape[1]
    across = jnp.broadcast_to(owner.astype(jnp.float32), (rows, rows))
    down = across.T
    first = lax.broadcasted_iota(jnp.int32, (rows, rows), 0)
    second = lax.broadcasted_iota(jnp.int32, (rows, rows), 1)
    earlier = jnp.where((across == down) & (first < second), 1, 0)
    return jnp.sum(earlier, axis=0, keepdims=True)


def place_kernel(swap_ref, owner_ref, integrals_ref, out_ref, both_ref, placed_ref, pick_ref, sem):
    rows, (lines, width) = integrals_ref.shape[0], out_ref.shape
    block = width // PLACE_STEPS
    fetches = [
        [
            pltpu.make_async_copy(
                integrals_ref.at[:, pl.ds(half * width + i * block, block)],
                both_ref.at[pl.ds(half * rows, rows), pl.ds(i * block, block)],
                sem.at[i, half],
            )
            for half in range(2)
        ]
        for i in range(PLACE_STEPS)
    ]
    for pair in fetches:
        for copy in pair:
            copy.start()

    owner = owner_ref[...]
    line = owner * BLOCK + slots_of(owner)
    number = lax.broadcasted_iota(jnp.int32, (lines, rows), 0)
    swap = swap_ref[0] * CAP
    pick_ref[:, :rows] = jnp.where(number == line + swap, 1.0, 0.0).astype(jnp.bfloat16)
    pick_ref[:, rows:] = jnp.where(number == line + (CAP - swap), 1.0, 0.0).astype(jnp.bfloat16)

    writes = []
    for i, pair in enumerate(fetches):
        for copy in pair:
            copy.wait()
        here = pl.ds(i * block, block)
        placed_ref[:, here] = jnp.dot(
            pick_ref[...], both_ref[:, here], preferred_element_type=jnp.float32
        ).astype(jnp.bfloat16)
        write = pltpu.make_async_copy(placed_ref.at[:, here], out_ref.at[:, here], sem.at[i, 2])
        write.start()
        writes.append(write)
    for write in writes:
        write.wait()


def place(swap, owner, integrals, peers):
    rows, cols = integrals.shape
    lines, width = peers * BLOCK, cols // 2
    return pl.pallas_call(
        place_kernel,
        in_specs=[whole_in(pltpu.SMEM), whole_in(pltpu.VMEM), whole_in(pl.ANY)],
        out_specs=whole_in(pl.ANY),
        out_shape=pltpu.HBM((lines, width), jnp.bfloat16),
        scratch_shapes=[
            pltpu.VMEM((2 * rows, width), jnp.bfloat16),
            pltpu.VMEM((lines, width), jnp.bfloat16),
            pltpu.VMEM((lines, 2 * rows), jnp.bfloat16),
            pltpu.SemaphoreType.DMA((PLACE_STEPS, 3)),
        ],
        compiler_params=pltpu.CompilerParams(vmem_limit_bytes=24 * 1024 * 1024),
        cost_estimate=pl.CostEstimate(
            flops=4 * lines * rows * width,
            bytes_accessed=2 * (2 * rows + lines) * width,
            transcendentals=0,
        ),
        name="place",
    )(swap, owner, pltpu.with_memory_space_constraint(integrals, pltpu.HBM))


def collect_kernel(amp_ref, mine_ref, left_ref, right_ref, top_ref, bottom_ref, out_ref, held_ref, sem):
    pairs = mine_ref.shape[0]
    count = out_ref.shape[0] // pairs
    shards = (
        (mine_ref, 0, 0),
        (left_ref, 1, 0),
        (right_ref, 3, 0),
        (top_ref, 2, 0),
        (bottom_ref, 2, pairs // 2),
    )
    fetches, writes = [], []
    for i, (ref, shift, skip) in enumerate(shards):
        at = (amp_ref[0] + count - shift) % count
        there = pl.ds(pl.multiple_of(at * pairs + skip, pairs // 2), ref.shape[0])
        fetches.append(pltpu.make_async_copy(ref, held_ref.at[there, :], sem.at[i, 0]))
        writes.append(
            pltpu.make_async_copy(held_ref.at[there, :], out_ref.at[there, :], sem.at[i, 1])
        )
    for copy in fetches:
        copy.start()
    for fetch, write in zip(fetches, writes):
        fetch.wait()
        write.start()
    for copy in writes:
        copy.wait()


def collect(amp, shards, count):
    pairs, cols = shards[0].shape
    return pl.pallas_call(
        collect_kernel,
        in_specs=[whole_in(pltpu.SMEM)] + [whole_in(pl.ANY)] * len(shards),
        out_specs=whole_in(pl.ANY),
        out_shape=pltpu.HBM((count * pairs, cols), jnp.bfloat16),
        scratch_shapes=[
            pltpu.VMEM((count * pairs, cols), jnp.bfloat16),
            pltpu.SemaphoreType.DMA((len(shards), 2)),
        ],
        compiler_params=pltpu.CompilerParams(vmem_limit_bytes=24 * 1024 * 1024),
        cost_estimate=pl.CostEstimate(
            flops=0, bytes_accessed=4 * count * pairs * cols, transcendentals=0
        ),
        name="collect",
    )(amp, *[pltpu.with_memory_space_constraint(x, pltpu.HBM) for x in shards])


def exchange(x, group):
    lines = x.shape[0]
    return jnp.where(group == 0, pltpu.roll(x, lines - CAP, 0), pltpu.roll(x, CAP, 0))


def multiply_kernel(rows_ref, amps_ref, out_ref, near_ref, held_ref, low_ref, high_ref, sem):
    lines, width = rows_ref.shape
    upper = lines // 2
    fetches, start = [], 0
    for i, block in enumerate(MULTIPLY_BLOCKS):
        fetches.append(
            [
                pltpu.make_async_copy(
                    source.at[:, pl.ds(first, block)], target.at[:, pl.ds(first, block)], sem.at[i, k]
                )
                for k, (source, target, first) in enumerate(
                    (
                        (rows_ref, near_ref, start),
                        (amps_ref, held_ref, start),
                        (amps_ref, held_ref, width + start),
                    )
                )
            ]
        )
        start += block
    for trio in fetches:
        for copy in trio:
            copy.start()

    start = 0
    for block, trio in zip(MULTIPLY_BLOCKS, fetches):
        for copy in trio:
            copy.wait()
        group = lax.broadcasted_iota(jnp.int32, (upper, block), 0) // CAP % 2
        here = pl.ds(start, block)
        first, second = near_ref[:upper, here], near_ref[upper:, here]
        for half, total_ref in enumerate((low_ref, high_ref)):
            product = lax.dot_general(
                jnp.where(group == half, first, second),
                held_ref[:, pl.ds(half * width + start, block)],
                (((1,), (1,)), ((), ())),
                preferred_element_type=jnp.float32,
            )
            if start == 0:
                total_ref[...] = product
            else:
                total_ref[...] += product
        start += block

    group = lax.broadcasted_iota(jnp.int32, low_ref.shape, 0) // CAP % 2
    value = low_ref[...] + exchange(high_ref[...], group)
    power = jnp.log2(jnp.maximum(jnp.max(jnp.abs(value), axis=1, keepdims=True), 2.0**-110))
    code = jnp.ceil(power * STEPS + 0.01).astype(jnp.int32)
    whole = jnp.round(value * (LARGEST / jnp.exp2(code.astype(jnp.float32) / STEPS)))
    whole = jnp.clip(whole, -LARGEST, LARGEST).astype(jnp.int32)
    whole = jnp.concatenate([whole, jnp.broadcast_to(code, (upper, LANES))], axis=1)
    blocks = whole.reshape(upper // BLOCK, 2, CAP, whole.shape[1])
    for j in range(2):
        first = j * (upper // BLOCK)
        out_ref[first : first + upper // BLOCK] = blocks[:, j].astype(jnp.int16)


def multiply(rows, amps):
    lines, width = rows.shape
    pairs = amps.shape[0]
    return pl.pallas_call(
        multiply_kernel,
        in_specs=[whole_in(pl.ANY)] * 2,
        out_specs=whole_in(pltpu.VMEM),
        out_shape=jax.ShapeDtypeStruct((lines // BLOCK, CAP, pairs + LANES), jnp.int16),
        scratch_shapes=[
            pltpu.VMEM((lines, width), jnp.bfloat16),
            pltpu.VMEM((pairs, 2 * width), jnp.bfloat16),
            pltpu.VMEM((lines // 2, pairs), jnp.float32),
            pltpu.VMEM((lines // 2, pairs), jnp.float32),
            pltpu.SemaphoreType.DMA((len(MULTIPLY_BLOCKS), 3)),
        ],
        compiler_params=pltpu.CompilerParams(vmem_limit_bytes=40 * 1024 * 1024),
        cost_estimate=pl.CostEstimate(
            flops=2 * lines * pairs * width,
            bytes_accessed=2 * (lines + 2 * pairs) * width,
            transcendentals=0,
        ),
        name="multiply",
    )(*[pltpu.with_memory_space_constraint(x, pltpu.HBM) for x in (rows, amps)])


def pick_kernel(owner_ref, lines_ref, out_ref):
    rows, pairs = out_ref.shape
    owner = owner_ref[...]
    line = owner * CAP + slots_of(owner)
    lines = lines_ref.shape[0] * CAP
    number = lax.broadcasted_iota(jnp.int32, (lines, rows), 0)
    pick = jnp.where(number == line, 1.0, 0.0).astype(jnp.bfloat16)
    whole = lines_ref[...].astype(jnp.int32).reshape(lines, lines_ref.shape[2])
    upper = whole >> 8
    lower = whole - (upper << 8)
    got = [
        lax.dot_general(
            pick,
            part.astype(jnp.float32).astype(jnp.bfloat16),
            (((0,), (0,)), ((), ())),
            preferred_element_type=jnp.float32,
        )
        for part in (upper, lower)
    ]
    picked = got[0] * 256.0 + got[1]
    unit = jnp.exp2(picked[:, pairs : pairs + 1] / STEPS) / LARGEST
    out_ref[...] = picked[:, :pairs] * unit


def pick(owner, lines):
    rows, pairs = owner.shape[1], lines.shape[2] - LANES
    return pl.pallas_call(
        pick_kernel,
        in_specs=[whole_in(pltpu.VMEM)] * 2,
        out_specs=whole_in(pltpu.VMEM),
        out_shape=jax.ShapeDtypeStruct((rows, pairs), jnp.float32),
        cost_estimate=pl.CostEstimate(
            flops=4 * rows * lines.size,
            bytes_accessed=2 * lines.size + 4 * rows * pairs,
            transcendentals=rows,
        ),
        name="pick",
    )(owner, lines)


def body(integrals, row_owner, lambda_amps):
    peers, amps = lax.axis_size("kblk"), lax.axis_size("amp")
    amp = lax.axis_index("amp").astype(jnp.int32)
    swap = (lax.axis_index("kblk") >= peers // 2).astype(jnp.int32)
    mine = lambda_amps[0]
    middle = mine.shape[0] // 2
    ahead = [(i, (i + 1) % amps) for i in range(amps)]
    back = [(i, (i - 1) % amps) for i in range(amps)]
    left, right = lax.ppermute(mine, "amp", ahead), lax.ppermute(mine, "amp", back)
    top = lax.ppermute(left[:middle], "amp", ahead)
    bottom = lax.ppermute(right[middle:], "amp", back)
    whole_lambda = collect(amp[None], (mine, left, right, top, bottom), amps)

    owner = row_owner.reshape(1, -1)
    placed = place(swap[None], owner, integrals, peers)
    width = placed.shape[1]
    arrived = lax.all_to_all(
        placed.reshape(peers, BLOCK, width), "kblk", split_axis=0, concat_axis=0, tiled=True
    )
    values = multiply(arrived.reshape(peers * BLOCK, width), whole_lambda)
    returned = lax.all_to_all(values, "kblk", split_axis=0, concat_axis=0, tiled=True)
    return pick(owner, returned)


def solution(mesh):
    placed = (P(("kblk", "amp"), None), P(("kblk", "amp"), None), P("kblk", "amp", None))
    return jax.shard_map(
        body, mesh=mesh, in_specs=placed, out_specs=P(("kblk", "amp"), None), check_vma=False
    )
```

```python
import jax
import jax.numpy as jnp
from jax import lax
from jax.experimental import pallas as pl
from jax.experimental.pallas import tpu as pltpu
from jax.sharding import PartitionSpec as P

CAP = 4
LARGEST = 32767.0
STEPS = 64
LANES = 128
BLOCK = 2 * CAP
PLACE_BLOCKS = (512, 1024, 1024, 1024, 1024, 1024, 1024, 1024, 512)
MULTIPLY_BLOCKS = (512, 1024, 1024, 1024, 1024, 1024, 1024, 1024, 512)
KEPT = 2


def whole_in(space):
    return pl.BlockSpec(memory_space=space)


def slots_of(owner):
    rows = owner.shape[1]
    across = jnp.broadcast_to(owner.astype(jnp.float32), (rows, rows))
    down = across.T
    first = lax.broadcasted_iota(jnp.int32, (rows, rows), 0)
    second = lax.broadcasted_iota(jnp.int32, (rows, rows), 1)
    earlier = jnp.where((across == down) & (first < second), 1, 0)
    return jnp.sum(earlier, axis=0, keepdims=True)


def place_kernel(swap_ref, owner_ref, integrals_ref, out_ref, both_ref, placed_ref, pick_ref, sem):
    rows, (lines, width) = integrals_ref.shape[0], out_ref.shape
    starts = [sum(PLACE_BLOCKS[:i]) for i in range(len(PLACE_BLOCKS))]
    fetches = [
        [
            pltpu.make_async_copy(
                integrals_ref.at[:, pl.ds(half * width + start, block)],
                both_ref.at[pl.ds(half * rows, rows), pl.ds(start, block)],
                sem.at[i, half],
            )
            for half in range(2)
        ]
        for i, (start, block) in enumerate(zip(starts, PLACE_BLOCKS))
    ]
    for pair in fetches:
        for copy in pair:
            copy.start()

    owner = owner_ref[...]
    line = owner * BLOCK + slots_of(owner)
    number = lax.broadcasted_iota(jnp.int32, (lines, rows), 0)
    swap = swap_ref[0] * CAP
    pick_ref[:, :rows] = jnp.where(number == line + swap, 1.0, 0.0).astype(jnp.bfloat16)
    pick_ref[:, rows:] = jnp.where(number == line + (CAP - swap), 1.0, 0.0).astype(jnp.bfloat16)

    writes = []
    for i, pair in enumerate(fetches):
        for copy in pair:
            copy.wait()
        here = pl.ds(starts[i], PLACE_BLOCKS[i])
        placed_ref[:, here] = jnp.dot(
            pick_ref[...], both_ref[:, here], preferred_element_type=jnp.float32
        ).astype(jnp.bfloat16)
        write = pltpu.make_async_copy(placed_ref.at[:, here], out_ref.at[:, here], sem.at[i, 2])
        write.start()
        writes.append(write)
    for write in writes:
        write.wait()


def place(swap, owner, integrals, peers):
    rows, cols = integrals.shape
    lines, width = peers * BLOCK, cols // 2
    return pl.pallas_call(
        place_kernel,
        in_specs=[whole_in(pltpu.SMEM), whole_in(pltpu.VMEM), whole_in(pl.ANY)],
        out_specs=whole_in(pl.ANY),
        out_shape=pltpu.HBM((lines, width), jnp.bfloat16),
        scratch_shapes=[
            pltpu.VMEM((2 * rows, width), jnp.bfloat16),
            pltpu.VMEM((lines, width), jnp.bfloat16),
            pltpu.VMEM((lines, 2 * rows), jnp.bfloat16),
            pltpu.SemaphoreType.DMA((len(PLACE_BLOCKS), 3)),
        ],
        compiler_params=pltpu.CompilerParams(vmem_limit_bytes=24 * 1024 * 1024),
        cost_estimate=pl.CostEstimate(
            flops=4 * lines * rows * width,
            bytes_accessed=2 * (2 * rows + lines) * width,
            transcendentals=0,
        ),
        name="place",
    )(swap, owner, pltpu.with_memory_space_constraint(integrals, pltpu.HBM))


def collect_kernel(
    amp_ref, owner_ref, mine_ref, left_ref, right_ref, top_ref, bottom_ref,
    out_ref, kept_ref, pick_ref, held_ref, sem,
):
    pairs = mine_ref.shape[0]
    count = out_ref.shape[0] // pairs
    shards = (
        (mine_ref, 0, 0),
        (left_ref, 1, 0),
        (right_ref, 3, 0),
        (top_ref, 2, 0),
        (bottom_ref, 2, pairs // 2),
    )
    fetches, writes = [], []
    for i, (ref, shift, skip) in enumerate(shards):
        at = (amp_ref[0] + count - shift) % count
        there = pl.ds(pl.multiple_of(at * pairs + skip, pairs // 2), ref.shape[0])
        fetches.append(pltpu.make_async_copy(ref, held_ref.at[there, :], sem.at[i, 0]))
        writes.append(
            pltpu.make_async_copy(held_ref.at[there, :], out_ref.at[there, :], sem.at[i, 1])
        )
    for copy in fetches:
        copy.start()
    owner = owner_ref[...]
    number = lax.broadcasted_iota(jnp.int32, pick_ref.shape, 0)
    here = number == owner * CAP + slots_of(owner)
    pick_ref[...] = jnp.where(here, 1.0, 0.0).astype(jnp.bfloat16)
    for fetch, write in zip(fetches, writes):
        fetch.wait()
        write.start()
    kept, width = kept_ref.shape[1] // 2, out_ref.shape[1] // 2
    kept_ref[:, :kept] = held_ref[:, :kept]
    kept_ref[:, kept:] = held_ref[:, width : width + kept]
    for copy in writes:
        copy.wait()


def collect(amp, owner, shards, count, peers):
    pairs, cols = shards[0].shape
    kept = 2 * sum(MULTIPLY_BLOCKS[:KEPT])
    return pl.pallas_call(
        collect_kernel,
        in_specs=[whole_in(pltpu.SMEM), whole_in(pltpu.VMEM)] + [whole_in(pl.ANY)] * len(shards),
        out_specs=[whole_in(pl.ANY), whole_in(pltpu.VMEM), whole_in(pltpu.VMEM)],
        out_shape=[
            pltpu.HBM((count * pairs, cols), jnp.bfloat16),
            pltpu.VMEM((count * pairs, kept), jnp.bfloat16),
            jax.ShapeDtypeStruct((peers * CAP, owner.shape[1]), jnp.bfloat16),
        ],
        scratch_shapes=[
            pltpu.VMEM((count * pairs, cols), jnp.bfloat16),
            pltpu.SemaphoreType.DMA((len(shards), 2)),
        ],
        compiler_params=pltpu.CompilerParams(vmem_limit_bytes=24 * 1024 * 1024),
        cost_estimate=pl.CostEstimate(
            flops=0, bytes_accessed=4 * count * pairs * cols, transcendentals=0
        ),
        name="collect",
    )(amp, owner, *[pltpu.with_memory_space_constraint(x, pltpu.HBM) for x in shards])


def exchange(x, group):
    lines = x.shape[0]
    return jnp.where(group == 0, pltpu.roll(x, lines - CAP, 0), pltpu.roll(x, CAP, 0))


def multiply_kernel(
    rows_ref, amps_ref, kept_ref, out_ref, near_ref, held_ref, low_ref, high_ref, sem
):
    lines, width = rows_ref.shape
    upper = lines // 2
    fetches, start = [], 0
    for i, block in enumerate(MULTIPLY_BLOCKS):
        fetches.append(
            [
                pltpu.make_async_copy(
                    source.at[:, pl.ds(first, block)], target.at[:, pl.ds(first, block)], sem.at[i, k]
                )
                for k, (source, target, first) in enumerate(
                    (
                        (rows_ref, near_ref, start),
                        (amps_ref, held_ref, start),
                        (amps_ref, held_ref, width + start),
                    )[: 1 if i < KEPT else 3]
                )
            ]
        )
        start += block
    for trio in fetches:
        for copy in trio:
            copy.start()

    start = 0
    for block, trio in zip(MULTIPLY_BLOCKS, fetches):
        for copy in trio:
            copy.wait()
        group = lax.broadcasted_iota(jnp.int32, (upper, block), 0) // CAP % 2
        here = pl.ds(start, block)
        first, second = near_ref[:upper, here], near_ref[upper:, here]
        kept = start < kept_ref.shape[1] // 2
        for half, total_ref in enumerate((low_ref, high_ref)):
            skip = half * (kept_ref.shape[1] // 2 if kept else width)
            product = lax.dot_general(
                jnp.where(group == half, first, second),
                (kept_ref if kept else held_ref)[:, pl.ds(skip + start, block)],
                (((1,), (1,)), ((), ())),
                preferred_element_type=jnp.float32,
            )
            if start == 0:
                total_ref[...] = product
            else:
                total_ref[...] += product
        start += block

    group = lax.broadcasted_iota(jnp.int32, low_ref.shape, 0) // CAP % 2
    value = low_ref[...] + exchange(high_ref[...], group)
    power = jnp.log2(jnp.maximum(jnp.max(jnp.abs(value), axis=1, keepdims=True), 2.0**-110))
    code = jnp.ceil(power * STEPS + 0.01).astype(jnp.int32)
    whole = jnp.round(value * (LARGEST / jnp.exp2(code.astype(jnp.float32) / STEPS)))
    whole = jnp.clip(whole, -LARGEST, LARGEST).astype(jnp.int32)
    whole = jnp.concatenate([whole, jnp.broadcast_to(code, (upper, LANES))], axis=1)
    blocks = whole.reshape(upper // BLOCK, 2, CAP, whole.shape[1])
    for j in range(2):
        first = j * (upper // BLOCK)
        out_ref[first : first + upper // BLOCK] = blocks[:, j].astype(jnp.int16)


def multiply(rows, amps, kept):
    lines, width = rows.shape
    pairs = amps.shape[0]
    return pl.pallas_call(
        multiply_kernel,
        in_specs=[whole_in(pl.ANY), whole_in(pl.ANY), whole_in(pltpu.VMEM)],
        out_specs=whole_in(pltpu.VMEM),
        out_shape=jax.ShapeDtypeStruct((lines // BLOCK, CAP, pairs + LANES), jnp.int16),
        scratch_shapes=[
            pltpu.VMEM((lines, width), jnp.bfloat16),
            pltpu.VMEM((pairs, 2 * width), jnp.bfloat16),
            pltpu.VMEM((lines // 2, pairs), jnp.float32),
            pltpu.VMEM((lines // 2, pairs), jnp.float32),
            pltpu.SemaphoreType.DMA((len(MULTIPLY_BLOCKS), 3)),
        ],
        compiler_params=pltpu.CompilerParams(vmem_limit_bytes=40 * 1024 * 1024),
        cost_estimate=pl.CostEstimate(
            flops=2 * lines * pairs * width,
            bytes_accessed=2 * (lines + 2 * pairs) * width,
            transcendentals=0,
        ),
        name="multiply",
    )(
        pltpu.with_memory_space_constraint(rows, pltpu.HBM),
        pltpu.with_memory_space_constraint(amps, pltpu.HBM),
        pltpu.with_memory_space_constraint(kept, pltpu.VMEM),
    )


def pick_kernel(pick_ref, lines_ref, out_ref):
    lines, pairs = pick_ref.shape[0], out_ref.shape[1]
    whole = lines_ref[...].astype(jnp.int32).reshape(lines, lines_ref.shape[2])
    upper = whole >> 8
    lower = whole - (upper << 8)
    got = [
        lax.dot_general(
            pick_ref[...],
            part.astype(jnp.float32).astype(jnp.bfloat16),
            (((0,), (0,)), ((), ())),
            preferred_element_type=jnp.float32,
        )
        for part in (upper, lower)
    ]
    picked = got[0] * 256.0 + got[1]
    unit = jnp.exp2(picked[:, pairs : pairs + 1] / STEPS) / LARGEST
    out_ref[...] = picked[:, :pairs] * unit


def pick(matrix, lines):
    rows, pairs = matrix.shape[1], lines.shape[2] - LANES
    return pl.pallas_call(
        pick_kernel,
        in_specs=[whole_in(pltpu.VMEM)] * 2,
        out_specs=whole_in(pltpu.VMEM),
        out_shape=jax.ShapeDtypeStruct((rows, pairs), jnp.float32),
        cost_estimate=pl.CostEstimate(
            flops=4 * rows * lines.size,
            bytes_accessed=2 * lines.size + 4 * rows * pairs,
            transcendentals=rows,
        ),
        name="pick",
    )(matrix, pltpu.with_memory_space_constraint(lines, pltpu.VMEM))


def body(integrals, row_owner, lambda_amps):
    peers, amps = lax.axis_size("kblk"), lax.axis_size("amp")
    amp = lax.axis_index("amp").astype(jnp.int32)
    swap = (lax.axis_index("kblk") >= peers // 2).astype(jnp.int32)
    mine = lambda_amps[0]
    middle = mine.shape[0] // 2
    ahead = [(i, (i + 1) % amps) for i in range(amps)]
    back = [(i, (i - 1) % amps) for i in range(amps)]
    left, right = lax.ppermute(mine, "amp", ahead), lax.ppermute(mine, "amp", back)
    top = lax.ppermute(left[:middle], "amp", ahead)
    bottom = lax.ppermute(right[middle:], "amp", back)
    owner = row_owner.reshape(1, -1)
    whole_lambda, kept, matrix = collect(
        amp[None], owner, (mine, left, right, top, bottom), amps, peers
    )

    placed = place(swap[None], owner, integrals, peers)
    width = placed.shape[1]
    arrived = lax.all_to_all(
        placed.reshape(peers, BLOCK, width), "kblk", split_axis=0, concat_axis=0, tiled=True
    )
    values = multiply(arrived.reshape(peers * BLOCK, width), whole_lambda, kept)
    returned = lax.all_to_all(values, "kblk", split_axis=0, concat_axis=0, tiled=True)
    return pick(matrix, returned)


def solution(mesh):
    placed = (P(("kblk", "amp"), None), P(("kblk", "amp"), None), P("kblk", "amp", None))
    return jax.shard_map(
        body, mesh=mesh, in_specs=placed, out_specs=P(("kblk", "amp"), None), check_vma=False
    )
```

```python
import jax
import jax.numpy as jnp
from jax import lax
from jax.experimental import pallas as pl
from jax.experimental.pallas import tpu as pltpu
from jax.sharding import PartitionSpec as P

CAP = 4
LARGEST = 32767.0
STEPS = 64
LANES = 128
BLOCK = 2 * CAP
PLACE_BLOCKS = (512, 1024, 1024, 1024, 1024, 1024, 1024, 1024, 512)
MULTIPLY_BLOCKS = (512, 1024, 1024, 1024, 1024, 1024, 1024, 1024, 256, 256)
KEPT = 2


def whole_in(space):
    return pl.BlockSpec(memory_space=space)


def slots_of(owner, upright=False):
    rows = owner.shape[1]
    across = jnp.broadcast_to(owner.astype(jnp.float32), (rows, rows))
    down = across.T
    first = lax.broadcasted_iota(jnp.int32, (rows, rows), 0)
    second = lax.broadcasted_iota(jnp.int32, (rows, rows), 1)
    if upright:
        earlier = jnp.where((across == down) & (second < first), 1, 0)
        return down[:, :1].astype(jnp.int32), jnp.sum(earlier, axis=1, keepdims=True)
    earlier = jnp.where((across == down) & (first < second), 1, 0)
    return jnp.sum(earlier, axis=0, keepdims=True)


def place_kernel(swap_ref, owner_ref, integrals_ref, out_ref, both_ref, placed_ref, pick_ref, sem):
    rows, (lines, width) = integrals_ref.shape[0], out_ref.shape
    starts = [sum(PLACE_BLOCKS[:i]) for i in range(len(PLACE_BLOCKS))]
    fetches = [
        [
            pltpu.make_async_copy(
                integrals_ref.at[:, pl.ds(half * width + start, block)],
                both_ref.at[pl.ds(half * rows, rows), pl.ds(start, block)],
                sem.at[i, half],
            )
            for half in range(2)
        ]
        for i, (start, block) in enumerate(zip(starts, PLACE_BLOCKS))
    ]
    for pair in fetches:
        for copy in pair:
            copy.start()

    owner = owner_ref[...]
    line = owner * BLOCK + slots_of(owner)
    number = lax.broadcasted_iota(jnp.int32, (lines, rows), 0)
    swap = swap_ref[0] * CAP
    pick_ref[:, :rows] = jnp.where(number == line + swap, 1.0, 0.0).astype(jnp.bfloat16)
    pick_ref[:, rows:] = jnp.where(number == line + (CAP - swap), 1.0, 0.0).astype(jnp.bfloat16)

    writes = []
    for i, pair in enumerate(fetches):
        for copy in pair:
            copy.wait()
        here = pl.ds(starts[i], PLACE_BLOCKS[i])
        placed_ref[:, here] = jnp.dot(
            pick_ref[...], both_ref[:, here], preferred_element_type=jnp.float32
        ).astype(jnp.bfloat16)
        write = pltpu.make_async_copy(placed_ref.at[:, here], out_ref.at[:, here], sem.at[i, 2])
        write.start()
        writes.append(write)
    for write in writes:
        write.wait()


def place(swap, owner, integrals, peers):
    rows, cols = integrals.shape
    lines, width = peers * BLOCK, cols // 2
    return pl.pallas_call(
        place_kernel,
        in_specs=[whole_in(pltpu.SMEM), whole_in(pltpu.VMEM), whole_in(pl.ANY)],
        out_specs=whole_in(pl.ANY),
        out_shape=pltpu.HBM((lines, width), jnp.bfloat16),
        scratch_shapes=[
            pltpu.VMEM((2 * rows, width), jnp.bfloat16),
            pltpu.VMEM((lines, width), jnp.bfloat16),
            pltpu.VMEM((lines, 2 * rows), jnp.bfloat16),
            pltpu.SemaphoreType.DMA((len(PLACE_BLOCKS), 3)),
        ],
        compiler_params=pltpu.CompilerParams(vmem_limit_bytes=24 * 1024 * 1024),
        cost_estimate=pl.CostEstimate(
            flops=4 * lines * rows * width,
            bytes_accessed=2 * (2 * rows + lines) * width,
            transcendentals=0,
        ),
        name="place",
    )(swap, owner, pltpu.with_memory_space_constraint(integrals, pltpu.HBM))


def collect_kernel(
    amp_ref, owner_ref, mine_ref, left_ref, right_ref, top_ref, bottom_ref,
    out_ref, kept_ref, pick_ref, held_ref, sem,
):
    pairs = mine_ref.shape[0]
    count = out_ref.shape[0] // pairs
    shards = (
        (mine_ref, 0, 0),
        (left_ref, 1, 0),
        (right_ref, 3, 0),
        (top_ref, 2, 0),
        (bottom_ref, 2, pairs // 2),
    )
    fetches, writes = [], []
    for i, (ref, shift, skip) in enumerate(shards):
        at = (amp_ref[0] + count - shift) % count
        there = pl.ds(pl.multiple_of(at * pairs + skip, pairs // 2), ref.shape[0])
        fetches.append(pltpu.make_async_copy(ref, held_ref.at[there, :], sem.at[i, 0]))
        writes.append(
            pltpu.make_async_copy(held_ref.at[there, :], out_ref.at[there, :], sem.at[i, 1])
        )
    for copy in fetches:
        copy.start()
    owner, slot = slots_of(owner_ref[...], upright=True)
    lines = pick_ref.shape[1] // 2
    number = lax.broadcasted_iota(jnp.int32, (pick_ref.shape[0], lines), 1)
    here = jnp.where(number == owner * CAP + slot, 1.0, 0.0)
    pick_ref[:, :lines] = (here * 256.0).astype(jnp.bfloat16)
    pick_ref[:, lines:] = here.astype(jnp.bfloat16)
    for fetch, write in zip(fetches, writes):
        fetch.wait()
        write.start()
    kept, width = kept_ref.shape[1] // 2, out_ref.shape[1] // 2
    kept_ref[:, :kept] = held_ref[:, :kept]
    kept_ref[:, kept:] = held_ref[:, width : width + kept]
    for copy in writes:
        copy.wait()


def collect(amp, owner, shards, count, peers):
    pairs, cols = shards[0].shape
    kept = 2 * sum(MULTIPLY_BLOCKS[:KEPT])
    return pl.pallas_call(
        collect_kernel,
        in_specs=[whole_in(pltpu.SMEM), whole_in(pltpu.VMEM)] + [whole_in(pl.ANY)] * len(shards),
        out_specs=[whole_in(pl.ANY), whole_in(pltpu.VMEM), whole_in(pltpu.VMEM)],
        out_shape=[
            pltpu.HBM((count * pairs, cols), jnp.bfloat16),
            pltpu.VMEM((count * pairs, kept), jnp.bfloat16),
            jax.ShapeDtypeStruct((owner.shape[1], 2 * peers * CAP), jnp.bfloat16),
        ],
        scratch_shapes=[
            pltpu.VMEM((count * pairs, cols), jnp.bfloat16),
            pltpu.SemaphoreType.DMA((len(shards), 2)),
        ],
        compiler_params=pltpu.CompilerParams(vmem_limit_bytes=24 * 1024 * 1024),
        cost_estimate=pl.CostEstimate(
            flops=0, bytes_accessed=4 * count * pairs * cols, transcendentals=0
        ),
        name="collect",
    )(amp, owner, *[pltpu.with_memory_space_constraint(x, pltpu.HBM) for x in shards])


def exchange(x, group):
    lines = x.shape[0]
    return jnp.where(group == 0, pltpu.roll(x, lines - CAP, 0), pltpu.roll(x, CAP, 0))


def multiply_kernel(
    rows_ref, amps_ref, kept_ref, out_ref, near_ref, held_ref, low_ref, high_ref, sem
):
    lines, width = rows_ref.shape
    upper = lines // 2
    fetches, start = [], 0
    for i, block in enumerate(MULTIPLY_BLOCKS):
        fetches.append(
            [
                pltpu.make_async_copy(
                    source.at[:, pl.ds(first, block)], target.at[:, pl.ds(first, block)], sem.at[i, k]
                )
                for k, (source, target, first) in enumerate(
                    (
                        (rows_ref, near_ref, start),
                        (amps_ref, held_ref, start),
                        (amps_ref, held_ref, width + start),
                    )[: 1 if i < KEPT else 3]
                )
            ]
        )
        start += block
    for trio in fetches:
        for copy in trio:
            copy.start()

    start = 0
    for block, trio in zip(MULTIPLY_BLOCKS, fetches):
        for copy in trio:
            copy.wait()
        group = lax.broadcasted_iota(jnp.int32, (upper, block), 0) // CAP % 2
        here = pl.ds(start, block)
        first, second = near_ref[:upper, here], near_ref[upper:, here]
        kept = start < kept_ref.shape[1] // 2
        for half, total_ref in enumerate((low_ref, high_ref)):
            skip = half * (kept_ref.shape[1] // 2 if kept else width)
            product = lax.dot_general(
                jnp.where(group == half, first, second),
                (kept_ref if kept else held_ref)[:, pl.ds(skip + start, block)],
                (((1,), (1,)), ((), ())),
                preferred_element_type=jnp.float32,
            )
            if start == 0:
                total_ref[...] = product
            else:
                total_ref[...] += product
        start += block

    group = lax.broadcasted_iota(jnp.int32, low_ref.shape, 0) // CAP % 2
    value = low_ref[...] + exchange(high_ref[...], group)
    power = jnp.log2(jnp.maximum(jnp.max(jnp.abs(value), axis=1, keepdims=True), 2.0**-110))
    code = jnp.ceil(power * STEPS + 0.01).astype(jnp.int32)
    whole = jnp.round(value * (LARGEST / jnp.exp2(code.astype(jnp.float32) / STEPS)))
    whole = jnp.clip(whole, -LARGEST, LARGEST).astype(jnp.int32)
    whole = jnp.concatenate([whole, jnp.broadcast_to(code, (upper, LANES))], axis=1)
    blocks = whole.reshape(upper // BLOCK, 2, CAP, whole.shape[1])
    for j in range(2):
        first = j * (upper // BLOCK)
        out_ref[first : first + upper // BLOCK] = blocks[:, j].astype(jnp.int16)


def multiply(rows, amps, kept):
    lines, width = rows.shape
    pairs = amps.shape[0]
    return pl.pallas_call(
        multiply_kernel,
        in_specs=[whole_in(pl.ANY), whole_in(pl.ANY), whole_in(pltpu.VMEM)],
        out_specs=whole_in(pltpu.VMEM),
        out_shape=jax.ShapeDtypeStruct((lines // BLOCK, CAP, pairs + LANES), jnp.int16),
        scratch_shapes=[
            pltpu.VMEM((lines, width), jnp.bfloat16),
            pltpu.VMEM((pairs, 2 * width), jnp.bfloat16),
            pltpu.VMEM((lines // 2, pairs), jnp.float32),
            pltpu.VMEM((lines // 2, pairs), jnp.float32),
            pltpu.SemaphoreType.DMA((len(MULTIPLY_BLOCKS), 3)),
        ],
        compiler_params=pltpu.CompilerParams(vmem_limit_bytes=40 * 1024 * 1024),
        cost_estimate=pl.CostEstimate(
            flops=2 * lines * pairs * width,
            bytes_accessed=2 * (lines + 2 * pairs) * width,
            transcendentals=0,
        ),
        name="multiply",
    )(
        pltpu.with_memory_space_constraint(rows, pltpu.HBM),
        pltpu.with_memory_space_constraint(amps, pltpu.HBM),
        pltpu.with_memory_space_constraint(kept, pltpu.VMEM),
    )


def pick_kernel(pick_ref, lines_ref, out_ref):
    lines, pairs = pick_ref.shape[1] // 2, out_ref.shape[1]
    whole = lines_ref[...].astype(jnp.int32).reshape(lines, lines_ref.shape[2])
    upper = whole >> 8
    parts = jnp.concatenate([upper, whole - (upper << 8)], axis=0)
    picked = jnp.dot(
        pick_ref[...],
        parts.astype(jnp.float32).astype(jnp.bfloat16),
        preferred_element_type=jnp.float32,
    )
    unit = jnp.exp2(picked[:, pairs : pairs + 1] / STEPS) / LARGEST
    out_ref[...] = picked[:, :pairs] * unit


def pick(matrix, lines):
    rows, pairs = matrix.shape[0], lines.shape[2] - LANES
    return pl.pallas_call(
        pick_kernel,
        in_specs=[whole_in(pltpu.VMEM)] * 2,
        out_specs=whole_in(pltpu.VMEM),
        out_shape=jax.ShapeDtypeStruct((rows, pairs), jnp.float32),
        cost_estimate=pl.CostEstimate(
            flops=4 * rows * lines.size,
            bytes_accessed=2 * lines.size + 4 * rows * pairs,
            transcendentals=rows,
        ),
        name="pick",
    )(matrix, pltpu.with_memory_space_constraint(lines, pltpu.VMEM))


def body(integrals, row_owner, lambda_amps):
    peers, amps = lax.axis_size("kblk"), lax.axis_size("amp")
    amp = lax.axis_index("amp").astype(jnp.int32)
    swap = (lax.axis_index("kblk") >= peers // 2).astype(jnp.int32)
    mine = lambda_amps[0]
    middle = mine.shape[0] // 2
    ahead = [(i, (i + 1) % amps) for i in range(amps)]
    back = [(i, (i - 1) % amps) for i in range(amps)]
    left, right = lax.ppermute(mine, "amp", ahead), lax.ppermute(mine, "amp", back)
    top = lax.ppermute(left[:middle], "amp", ahead)
    bottom = lax.ppermute(right[middle:], "amp", back)
    owner = row_owner.reshape(1, -1)
    whole_lambda, kept, matrix = collect(
        amp[None], owner, (mine, left, right, top, bottom), amps, peers
    )

    placed = place(swap[None], owner, integrals, peers)
    width = placed.shape[1]
    arrived = lax.all_to_all(
        placed.reshape(peers, BLOCK, width), "kblk", split_axis=0, concat_axis=0, tiled=True
    )
    values = multiply(arrived.reshape(peers * BLOCK, width), whole_lambda, kept)
    returned = lax.all_to_all(values, "kblk", split_axis=0, concat_axis=0, tiled=True)
    return pick(matrix, returned)


def solution(mesh):
    placed = (P(("kblk", "amp"), None), P(("kblk", "amp"), None), P("kblk", "amp", None))
    return jax.shard_map(
        body, mesh=mesh, in_specs=placed, out_specs=P(("kblk", "amp"), None), check_vma=False
    )
```

```python
import jax
import jax.numpy as jnp
from jax import lax
from jax.experimental import pallas as pl
from jax.experimental.pallas import tpu as pltpu
from jax.sharding import PartitionSpec as P

CAP = 4
LARGEST = 32767.0
STEPS = 64
LANES = 128
BLOCK = 2 * CAP
PLACE_BLOCKS = (512, 1024, 1024, 1024, 1024, 1024, 1024, 1024, 512)
MULTIPLY_BLOCKS = (512, 1024, 1024, 1024, 1024, 1024, 1024, 1024, 256, 256)
KEPT = 2


def whole_in(space):
    return pl.BlockSpec(memory_space=space)


def slots_of(owner, upright=False):
    rows = owner.shape[1]
    across = jnp.broadcast_to(owner.astype(jnp.float32), (rows, rows))
    down = across.T
    first = lax.broadcasted_iota(jnp.int32, (rows, rows), 0)
    second = lax.broadcasted_iota(jnp.int32, (rows, rows), 1)
    if upright:
        earlier = jnp.where((across == down) & (second < first), 1, 0)
        return down[:, :1].astype(jnp.int32), jnp.sum(earlier, axis=1, keepdims=True)
    earlier = jnp.where((across == down) & (first < second), 1, 0)
    return jnp.sum(earlier, axis=0, keepdims=True)


def place_kernel(swap_ref, owner_ref, integrals_ref, out_ref, both_ref, placed_ref, pick_ref, sem):
    rows, (lines, width) = integrals_ref.shape[0], out_ref.shape
    starts = [sum(PLACE_BLOCKS[:i]) for i in range(len(PLACE_BLOCKS))]
    fetches = [
        [
            pltpu.make_async_copy(
                integrals_ref.at[:, pl.ds(half * width + start, block)],
                both_ref.at[pl.ds(half * rows, rows), pl.ds(start, block)],
                sem.at[i, half],
            )
            for half in range(2)
        ]
        for i, (start, block) in enumerate(zip(starts, PLACE_BLOCKS))
    ]
    for pair in fetches:
        for copy in pair:
            copy.start()

    owner = owner_ref[...]
    line = owner * BLOCK + slots_of(owner)
    number = lax.broadcasted_iota(jnp.int32, (lines, rows), 0)
    swap = swap_ref[0] * CAP
    pick_ref[:, :rows] = jnp.where(number == line + swap, 1.0, 0.0).astype(jnp.bfloat16)
    pick_ref[:, rows:] = jnp.where(number == line + (CAP - swap), 1.0, 0.0).astype(jnp.bfloat16)

    writes = []
    for i, pair in enumerate(fetches):
        for copy in pair:
            copy.wait()
        here = pl.ds(starts[i], PLACE_BLOCKS[i])
        placed_ref[:, here] = jnp.dot(
            pick_ref[...], both_ref[:, here], preferred_element_type=jnp.float32
        ).astype(jnp.bfloat16)
        write = pltpu.make_async_copy(placed_ref.at[:, here], out_ref.at[:, here], sem.at[i, 2])
        write.start()
        writes.append(write)
    for write in writes:
        write.wait()


def place(swap, owner, integrals, peers):
    rows, cols = integrals.shape
    lines, width = peers * BLOCK, cols // 2
    return pl.pallas_call(
        place_kernel,
        in_specs=[whole_in(pltpu.SMEM), whole_in(pltpu.VMEM), whole_in(pl.ANY)],
        out_specs=whole_in(pl.ANY),
        out_shape=pltpu.HBM((lines, width), jnp.bfloat16),
        scratch_shapes=[
            pltpu.VMEM((2 * rows, width), jnp.bfloat16),
            pltpu.VMEM((lines, width), jnp.bfloat16),
            pltpu.VMEM((lines, 2 * rows), jnp.bfloat16),
            pltpu.SemaphoreType.DMA((len(PLACE_BLOCKS), 3)),
        ],
        compiler_params=pltpu.CompilerParams(vmem_limit_bytes=24 * 1024 * 1024),
        cost_estimate=pl.CostEstimate(
            flops=4 * lines * rows * width,
            bytes_accessed=2 * (2 * rows + lines) * width,
            transcendentals=0,
        ),
        name="place",
    )(swap, owner, pltpu.with_memory_space_constraint(integrals, pltpu.HBM))


def collect_kernel(
    amp_ref, owner_ref, mine_ref, left_ref, right_ref, top_ref, bottom_ref,
    out_ref, kept_ref, pick_ref, held_ref, sem,
):
    pairs = mine_ref.shape[0]
    count = out_ref.shape[0] // pairs
    shards = (
        (mine_ref, 0, 0),
        (left_ref, 1, 0),
        (right_ref, 3, 0),
        (top_ref, 2, 0),
        (bottom_ref, 2, pairs // 2),
    )
    fetches, writes = [], []
    for i, (ref, shift, skip) in enumerate(shards):
        at = (amp_ref[0] + count - shift) % count
        there = pl.ds(pl.multiple_of(at * pairs + skip, pairs // 2), ref.shape[0])
        fetches.append(pltpu.make_async_copy(ref, held_ref.at[there, :], sem.at[i, 0]))
        writes.append(
            pltpu.make_async_copy(held_ref.at[there, :], out_ref.at[there, :], sem.at[i, 1])
        )
    for copy in fetches:
        copy.start()
    owner, slot = slots_of(owner_ref[...], upright=True)
    lines = pick_ref.shape[1] // 2
    number = lax.broadcasted_iota(jnp.int32, (pick_ref.shape[0], lines), 1)
    here = jnp.where(number == owner * CAP + slot, 1.0, 0.0)
    pick_ref[:, :lines] = (here * 256.0).astype(jnp.bfloat16)
    pick_ref[:, lines:] = here.astype(jnp.bfloat16)
    for fetch, write in zip(fetches, writes):
        fetch.wait()
        write.start()
    kept, width = kept_ref.shape[1] // 2, out_ref.shape[1] // 2
    kept_ref[:, :kept] = held_ref[:, :kept]
    kept_ref[:, kept:] = held_ref[:, width : width + kept]
    for copy in writes:
        copy.wait()


def collect(amp, owner, shards, count, peers):
    pairs, cols = shards[0].shape
    kept = 2 * sum(MULTIPLY_BLOCKS[:KEPT])
    return pl.pallas_call(
        collect_kernel,
        in_specs=[whole_in(pltpu.SMEM), whole_in(pltpu.VMEM)] + [whole_in(pl.ANY)] * len(shards),
        out_specs=[whole_in(pl.ANY), whole_in(pltpu.VMEM), whole_in(pltpu.VMEM)],
        out_shape=[
            pltpu.HBM((count * pairs, cols), jnp.bfloat16),
            pltpu.VMEM((count * pairs, kept), jnp.bfloat16),
            jax.ShapeDtypeStruct((owner.shape[1], 2 * peers * CAP), jnp.bfloat16),
        ],
        scratch_shapes=[
            pltpu.VMEM((count * pairs, cols), jnp.bfloat16),
            pltpu.SemaphoreType.DMA((len(shards), 2)),
        ],
        compiler_params=pltpu.CompilerParams(vmem_limit_bytes=24 * 1024 * 1024),
        cost_estimate=pl.CostEstimate(
            flops=0, bytes_accessed=4 * count * pairs * cols, transcendentals=0
        ),
        name="collect",
    )(amp, owner, *[pltpu.with_memory_space_constraint(x, pltpu.HBM) for x in shards])


def exchange(x, group):
    lines = x.shape[0]
    return jnp.where(group == 0, pltpu.roll(x, lines - CAP, 0), pltpu.roll(x, CAP, 0))


def multiply_kernel(
    rows_ref, amps_ref, kept_ref, out_ref, near_ref, held_ref, low_ref, high_ref, sem
):
    lines, width = rows_ref.shape
    upper = lines // 2
    fetches, start = [], 0
    for i, block in enumerate(MULTIPLY_BLOCKS):
        fetches.append(
            [
                pltpu.make_async_copy(
                    source.at[:, pl.ds(first, block)], target.at[:, pl.ds(first, block)], sem.at[i, k]
                )
                for k, (source, target, first) in enumerate(
                    (
                        (rows_ref, near_ref, start),
                        (amps_ref, held_ref, start),
                        (amps_ref, held_ref, width + start),
                    )[: 1 if i < KEPT else 3]
                )
            ]
        )
        start += block
    for trio in fetches:
        for copy in trio:
            copy.start()

    start = 0
    for block, trio in zip(MULTIPLY_BLOCKS, fetches):
        for copy in trio:
            copy.wait()
        group = lax.broadcasted_iota(jnp.int32, (upper, block), 0) // CAP % 2
        here = pl.ds(start, block)
        first, second = near_ref[:upper, here], near_ref[upper:, here]
        kept = start < kept_ref.shape[1] // 2
        for half, total_ref in enumerate((low_ref, high_ref)):
            skip = half * (kept_ref.shape[1] // 2 if kept else width)
            product = lax.dot_general(
                (kept_ref if kept else held_ref)[:, pl.ds(skip + start, block)],
                jnp.where(group == half, first, second),
                (((1,), (1,)), ((), ())),
                preferred_element_type=jnp.float32,
            )
            if start == 0:
                total_ref[...] = product
            else:
                total_ref[...] += product
        start += block

    low, high = low_ref[...].T, high_ref[...].T
    group = lax.broadcasted_iota(jnp.int32, low.shape, 0) // CAP % 2
    value = low + exchange(high, group)
    power = jnp.log2(jnp.maximum(jnp.max(jnp.abs(value), axis=1, keepdims=True), 2.0**-110))
    code = jnp.ceil(power * STEPS + 0.01).astype(jnp.int32)
    whole = jnp.round(value * (LARGEST / jnp.exp2(code.astype(jnp.float32) / STEPS)))
    whole = jnp.clip(whole, -LARGEST, LARGEST).astype(jnp.int32)
    whole = jnp.concatenate([whole, jnp.broadcast_to(code, (upper, LANES))], axis=1)
    blocks = whole.reshape(upper // BLOCK, 2, CAP, whole.shape[1])
    for j in range(2):
        first = j * (upper // BLOCK)
        out_ref[first : first + upper // BLOCK] = blocks[:, j].astype(jnp.int16)


def multiply(rows, amps, kept):
    lines, width = rows.shape
    pairs = amps.shape[0]
    return pl.pallas_call(
        multiply_kernel,
        in_specs=[whole_in(pl.ANY), whole_in(pl.ANY), whole_in(pltpu.VMEM)],
        out_specs=whole_in(pltpu.VMEM),
        out_shape=jax.ShapeDtypeStruct((lines // BLOCK, CAP, pairs + LANES), jnp.int16),
        scratch_shapes=[
            pltpu.VMEM((lines, width), jnp.bfloat16),
            pltpu.VMEM((pairs, 2 * width), jnp.bfloat16),
            pltpu.VMEM((pairs, lines // 2), jnp.float32),
            pltpu.VMEM((pairs, lines // 2), jnp.float32),
            pltpu.SemaphoreType.DMA((len(MULTIPLY_BLOCKS), 3)),
        ],
        compiler_params=pltpu.CompilerParams(vmem_limit_bytes=40 * 1024 * 1024),
        cost_estimate=pl.CostEstimate(
            flops=2 * lines * pairs * width,
            bytes_accessed=2 * (lines + 2 * pairs) * width,
            transcendentals=0,
        ),
        name="multiply",
    )(
        pltpu.with_memory_space_constraint(rows, pltpu.HBM),
        pltpu.with_memory_space_constraint(amps, pltpu.HBM),
        pltpu.with_memory_space_constraint(kept, pltpu.VMEM),
    )


def pick_kernel(pick_ref, lines_ref, out_ref):
    lines, pairs = pick_ref.shape[1] // 2, out_ref.shape[1]
    whole = lines_ref[...].astype(jnp.int32).reshape(lines, lines_ref.shape[2])
    upper = whole >> 8
    parts = jnp.concatenate([upper, whole - (upper << 8)], axis=0)
    picked = jnp.dot(
        pick_ref[...],
        parts.astype(jnp.float32).astype(jnp.bfloat16),
        preferred_element_type=jnp.float32,
    )
    unit = jnp.exp2(picked[:, pairs : pairs + 1] / STEPS) / LARGEST
    out_ref[...] = picked[:, :pairs] * unit


def pick(matrix, lines):
    rows, pairs = matrix.shape[0], lines.shape[2] - LANES
    return pl.pallas_call(
        pick_kernel,
        in_specs=[whole_in(pltpu.VMEM)] * 2,
        out_specs=whole_in(pltpu.VMEM),
        out_shape=jax.ShapeDtypeStruct((rows, pairs), jnp.float32),
        cost_estimate=pl.CostEstimate(
            flops=4 * rows * lines.size,
            bytes_accessed=2 * lines.size + 4 * rows * pairs,
            transcendentals=rows,
        ),
        name="pick",
    )(matrix, pltpu.with_memory_space_constraint(lines, pltpu.VMEM))


def body(integrals, row_owner, lambda_amps):
    peers, amps = lax.axis_size("kblk"), lax.axis_size("amp")
    amp = lax.axis_index("amp").astype(jnp.int32)
    swap = (lax.axis_index("kblk") >= peers // 2).astype(jnp.int32)
    mine = lambda_amps[0]
    middle = mine.shape[0] // 2
    ahead = [(i, (i + 1) % amps) for i in range(amps)]
    back = [(i, (i - 1) % amps) for i in range(amps)]
    left, right = lax.ppermute(mine, "amp", ahead), lax.ppermute(mine, "amp", back)
    top = lax.ppermute(left[:middle], "amp", ahead)
    bottom = lax.ppermute(right[middle:], "amp", back)
    owner = row_owner.reshape(1, -1)
    whole_lambda, kept, matrix = collect(
        amp[None], owner, (mine, left, right, top, bottom), amps, peers
    )

    placed = place(swap[None], owner, integrals, peers)
    width = placed.shape[1]
    arrived = lax.all_to_all(
        placed.reshape(peers, BLOCK, width), "kblk", split_axis=0, concat_axis=0, tiled=True
    )
    values = multiply(arrived.reshape(peers * BLOCK, width), whole_lambda, kept)
    returned = lax.all_to_all(values, "kblk", split_axis=0, concat_axis=0, tiled=True)
    return pick(matrix, returned)


def solution(mesh):
    placed = (P(("kblk", "amp"), None), P(("kblk", "amp"), None), P("kblk", "amp", None))
    return jax.shard_map(
        body, mesh=mesh, in_specs=placed, out_specs=P(("kblk", "amp"), None), check_vma=False
    )
```

```python
import jax
import jax.numpy as jnp
from jax import lax
from jax.experimental import pallas as pl
from jax.experimental.pallas import tpu as pltpu
from jax.sharding import PartitionSpec as P

CAP = 4
LARGEST = 32767.0
STEPS = 64
LANES = 128
BLOCK = 2 * CAP
PLACE_STEPS = 8
MULTIPLY_BLOCK = 1024
HEAD = 1536


def whole_in(space):
    return pl.BlockSpec(memory_space=space)


def slots_of(owner, upright=False):
    rows = owner.shape[1]
    across = jnp.broadcast_to(owner.astype(jnp.float32), (rows, rows))
    down = across.T
    first = lax.broadcasted_iota(jnp.int32, (rows, rows), 0)
    second = lax.broadcasted_iota(jnp.int32, (rows, rows), 1)
    if upright:
        earlier = jnp.where((across == down) & (second < first), 1, 0)
        return down[:, :1].astype(jnp.int32), jnp.sum(earlier, axis=1, keepdims=True)
    earlier = jnp.where((across == down) & (first < second), 1, 0)
    return jnp.sum(earlier, axis=0, keepdims=True)


def place_kernel(swap_ref, owner_ref, integrals_ref, out_ref, both_ref, placed_ref, pick_ref, sem):
    rows, (lines, width) = integrals_ref.shape[0], out_ref.shape
    block = width // PLACE_STEPS

    def columns(i, half=0):
        return pl.ds(pl.multiple_of(half * width + i * block, block), block)

    def fetch(i, half):
        return pltpu.make_async_copy(
            integrals_ref.at[:, columns(i, half)],
            both_ref.at[pl.ds(half * rows, rows), columns(i)],
            sem.at[i, half],
        )

    def write(i):
        return pltpu.make_async_copy(
            placed_ref.at[:, columns(i)], out_ref.at[:, columns(i)], sem.at[i, 2]
        )

    @pl.loop(0, PLACE_STEPS)
    def _(i):
        fetch(i, 0).start()
        fetch(i, 1).start()

    owner = owner_ref[...]
    line = owner * BLOCK + slots_of(owner)
    number = lax.broadcasted_iota(jnp.int32, (lines, rows), 0)
    swap = swap_ref[0] * CAP
    pick_ref[:, :rows] = jnp.where(number == line + swap, 1.0, 0.0).astype(jnp.bfloat16)
    pick_ref[:, rows:] = jnp.where(number == line + (CAP - swap), 1.0, 0.0).astype(jnp.bfloat16)

    @pl.loop(0, PLACE_STEPS)
    def _(i):
        fetch(i, 0).wait()
        fetch(i, 1).wait()
        placed_ref[:, columns(i)] = jnp.dot(
            pick_ref[...], both_ref[:, columns(i)], preferred_element_type=jnp.float32
        ).astype(jnp.bfloat16)
        write(i).start()

    @pl.loop(0, PLACE_STEPS)
    def _(i):
        write(i).wait()


def place(swap, owner, integrals, peers):
    rows, cols = integrals.shape
    lines, width = peers * BLOCK, cols // 2
    return pl.pallas_call(
        place_kernel,
        in_specs=[whole_in(pltpu.SMEM), whole_in(pltpu.VMEM), whole_in(pl.ANY)],
        out_specs=whole_in(pl.ANY),
        out_shape=pltpu.HBM((lines, width), jnp.bfloat16),
        scratch_shapes=[
            pltpu.VMEM((2 * rows, width), jnp.bfloat16),
            pltpu.VMEM((lines, width), jnp.bfloat16),
            pltpu.VMEM((lines, 2 * rows), jnp.bfloat16),
            pltpu.SemaphoreType.DMA((PLACE_STEPS, 3)),
        ],
        compiler_params=pltpu.CompilerParams(vmem_limit_bytes=24 * 1024 * 1024),
        cost_estimate=pl.CostEstimate(
            flops=4 * lines * rows * width,
            bytes_accessed=2 * (2 * rows + lines) * width,
            transcendentals=0,
        ),
        name="place",
    )(swap, owner, pltpu.with_memory_space_constraint(integrals, pltpu.HBM))


def collect_kernel(
    amp_ref, owner_ref, mine_ref, left_ref, right_ref, top_ref, bottom_ref,
    out_ref, kept_ref, pick_ref, held_ref, sem,
):
    pairs = mine_ref.shape[0]
    count = out_ref.shape[0] // pairs
    shards = (
        (mine_ref, 0, 0),
        (left_ref, 1, 0),
        (right_ref, 3, 0),
        (top_ref, 2, 0),
        (bottom_ref, 2, pairs // 2),
    )
    fetches, writes = [], []
    for i, (ref, shift, skip) in enumerate(shards):
        at = (amp_ref[0] + count - shift) % count
        there = pl.ds(pl.multiple_of(at * pairs + skip, pairs // 2), ref.shape[0])
        fetches.append(pltpu.make_async_copy(ref, held_ref.at[there, :], sem.at[i, 0]))
        writes.append(
            pltpu.make_async_copy(held_ref.at[there, :], out_ref.at[there, :], sem.at[i, 1])
        )
    for copy in fetches:
        copy.start()
    owner, slot = slots_of(owner_ref[...], upright=True)
    lines = pick_ref.shape[1] // 2
    number = lax.broadcasted_iota(jnp.int32, (pick_ref.shape[0], lines), 1)
    here = jnp.where(number == owner * CAP + slot, 1.0, 0.0)
    pick_ref[:, :lines] = (here * 256.0).astype(jnp.bfloat16)
    pick_ref[:, lines:] = here.astype(jnp.bfloat16)
    for fetch, write in zip(fetches, writes):
        fetch.wait()
        write.start()
    kept, width = kept_ref.shape[1] // 2, out_ref.shape[1] // 2
    kept_ref[:, :kept] = held_ref[:, :kept]
    kept_ref[:, kept:] = held_ref[:, width : width + kept]
    for copy in writes:
        copy.wait()


def collect(amp, owner, shards, count, peers):
    pairs, cols = shards[0].shape
    kept = 2 * HEAD
    return pl.pallas_call(
        collect_kernel,
        in_specs=[whole_in(pltpu.SMEM), whole_in(pltpu.VMEM)] + [whole_in(pl.ANY)] * len(shards),
        out_specs=[whole_in(pl.ANY), whole_in(pltpu.VMEM), whole_in(pltpu.VMEM)],
        out_shape=[
            pltpu.HBM((count * pairs, cols), jnp.bfloat16),
            pltpu.VMEM((count * pairs, kept), jnp.bfloat16),
            jax.ShapeDtypeStruct((owner.shape[1], 2 * peers * CAP), jnp.bfloat16),
        ],
        scratch_shapes=[
            pltpu.VMEM((count * pairs, cols), jnp.bfloat16),
            pltpu.SemaphoreType.DMA((len(shards), 2)),
        ],
        compiler_params=pltpu.CompilerParams(vmem_limit_bytes=24 * 1024 * 1024),
        cost_estimate=pl.CostEstimate(
            flops=0, bytes_accessed=4 * count * pairs * cols, transcendentals=0
        ),
        name="collect",
    )(amp, owner, *[pltpu.with_memory_space_constraint(x, pltpu.HBM) for x in shards])


def exchange(x, group):
    lines = x.shape[0]
    return jnp.where(group == 0, pltpu.roll(x, lines - CAP, 0), pltpu.roll(x, CAP, 0))


def multiply_kernel(
    rows_ref, amps_ref, kept_ref, out_ref, near_ref, held_ref, low_ref, high_ref, sem
):
    lines, width = rows_ref.shape
    upper = lines // 2
    steps = (width - HEAD) // MULTIPLY_BLOCK
    tail = HEAD + steps * MULTIPLY_BLOCK

    def fetches(i, start, block, halves=2):
        at = [pl.ds(half * width + start, block) for half in range(2)]
        copies = [pltpu.make_async_copy(rows_ref.at[:, at[0]], near_ref.at[:, at[0]], sem.at[i, 0])]
        for half in range(halves):
            copies.append(
                pltpu.make_async_copy(
                    amps_ref.at[:, at[half]], held_ref.at[:, at[half]], sem.at[i, 1 + half]
                )
            )
        return copies

    def middle(i):
        start = pl.multiple_of(HEAD + i * MULTIPLY_BLOCK, 512)
        return fetches(1 + i, start, MULTIPLY_BLOCK), start

    def work(start, block, table_ref, half_width):
        group = lax.broadcasted_iota(jnp.int32, (upper, block), 0) // CAP % 2
        first, second = near_ref[:upper, pl.ds(start, block)], near_ref[upper:, pl.ds(start, block)]
        for half, total_ref in enumerate((low_ref, high_ref)):
            total_ref[...] += lax.dot_general(
                jnp.where(group == half, first, second),
                table_ref[:, pl.ds(half * half_width + start, block)],
                (((1,), (1,)), ((), ())),
                preferred_element_type=jnp.float32,
            )

    head = fetches(0, 0, HEAD, 0)[0]
    head.start()

    @pl.loop(0, steps)
    def _(i):
        for copy in middle(i)[0]:
            copy.start()

    rest = fetches(1 + steps, tail, width - tail)
    for copy in rest:
        copy.start()
    low_ref[...] = jnp.zeros_like(low_ref)
    high_ref[...] = jnp.zeros_like(high_ref)
    head.wait()
    work(0, HEAD, kept_ref, HEAD)

    @pl.loop(0, steps)
    def _(i):
        copies, start = middle(i)
        for copy in copies:
            copy.wait()
        work(start, MULTIPLY_BLOCK, held_ref, width)

    for copy in rest:
        copy.wait()
    work(tail, width - tail, held_ref, width)

    group = lax.broadcasted_iota(jnp.int32, low_ref.shape, 0) // CAP % 2
    value = low_ref[...] + exchange(high_ref[...], group)
    power = jnp.log2(jnp.maximum(jnp.max(jnp.abs(value), axis=1, keepdims=True), 2.0**-110))
    code = jnp.ceil(power * STEPS + 0.01).astype(jnp.int32)
    whole = jnp.round(value * (LARGEST / jnp.exp2(code.astype(jnp.float32) / STEPS)))
    whole = jnp.clip(whole, -LARGEST, LARGEST).astype(jnp.int32)
    whole = jnp.concatenate([whole, jnp.broadcast_to(code, (upper, LANES))], axis=1)
    blocks = whole.reshape(upper // BLOCK, 2, CAP, whole.shape[1])
    for j in range(2):
        first = j * (upper // BLOCK)
        out_ref[first : first + upper // BLOCK] = blocks[:, j].astype(jnp.int16)


def multiply(rows, amps, kept):
    lines, width = rows.shape
    pairs = amps.shape[0]
    return pl.pallas_call(
        multiply_kernel,
        in_specs=[whole_in(pl.ANY), whole_in(pl.ANY), whole_in(pltpu.VMEM)],
        out_specs=whole_in(pltpu.VMEM),
        out_shape=jax.ShapeDtypeStruct((lines // BLOCK, CAP, pairs + LANES), jnp.int16),
        scratch_shapes=[
            pltpu.VMEM((lines, width), jnp.bfloat16),
            pltpu.VMEM((pairs, 2 * width), jnp.bfloat16),
            pltpu.VMEM((lines // 2, pairs), jnp.float32),
            pltpu.VMEM((lines // 2, pairs), jnp.float32),
            pltpu.SemaphoreType.DMA((2 + (width - HEAD) // MULTIPLY_BLOCK, 3)),
        ],
        compiler_params=pltpu.CompilerParams(vmem_limit_bytes=40 * 1024 * 1024),
        cost_estimate=pl.CostEstimate(
            flops=2 * lines * pairs * width,
            bytes_accessed=2 * (lines + 2 * pairs) * width,
            transcendentals=0,
        ),
        name="multiply",
    )(
        pltpu.with_memory_space_constraint(rows, pltpu.HBM),
        pltpu.with_memory_space_constraint(amps, pltpu.HBM),
        pltpu.with_memory_space_constraint(kept, pltpu.VMEM),
    )


def pick_kernel(pick_ref, lines_ref, out_ref):
    lines, pairs = pick_ref.shape[1] // 2, out_ref.shape[1]
    whole = lines_ref[...].astype(jnp.int32).reshape(lines, lines_ref.shape[2])
    upper = whole >> 8
    parts = jnp.concatenate([upper, whole - (upper << 8)], axis=0)
    picked = jnp.dot(
        pick_ref[...],
        parts.astype(jnp.float32).astype(jnp.bfloat16),
        preferred_element_type=jnp.float32,
    )
    unit = jnp.exp2(picked[:, pairs : pairs + 1] / STEPS) / LARGEST
    out_ref[...] = picked[:, :pairs] * unit


def pick(matrix, lines):
    rows, pairs = matrix.shape[0], lines.shape[2] - LANES
    return pl.pallas_call(
        pick_kernel,
        in_specs=[whole_in(pltpu.VMEM)] * 2,
        out_specs=whole_in(pltpu.VMEM),
        out_shape=jax.ShapeDtypeStruct((rows, pairs), jnp.float32),
        cost_estimate=pl.CostEstimate(
            flops=4 * rows * lines.size,
            bytes_accessed=2 * lines.size + 4 * rows * pairs,
            transcendentals=rows,
        ),
        name="pick",
    )(matrix, pltpu.with_memory_space_constraint(lines, pltpu.VMEM))


def body(integrals, row_owner, lambda_amps):
    peers, amps = lax.axis_size("kblk"), lax.axis_size("amp")
    amp = lax.axis_index("amp").astype(jnp.int32)
    swap = (lax.axis_index("kblk") >= peers // 2).astype(jnp.int32)
    mine = lambda_amps[0]
    middle = mine.shape[0] // 2
    ahead = [(i, (i + 1) % amps) for i in range(amps)]
    back = [(i, (i - 1) % amps) for i in range(amps)]
    left, right = lax.ppermute(mine, "amp", ahead), lax.ppermute(mine, "amp", back)
    top = lax.ppermute(left[:middle], "amp", ahead)
    bottom = lax.ppermute(right[middle:], "amp", back)
    owner = row_owner.reshape(1, -1)
    whole_lambda, kept, matrix = collect(
        amp[None], owner, (mine, left, right, top, bottom), amps, peers
    )

    placed = place(swap[None], owner, integrals, peers)
    width = placed.shape[1]
    arrived = lax.all_to_all(
        placed.reshape(peers, BLOCK, width), "kblk", split_axis=0, concat_axis=0, tiled=True
    )
    values = multiply(arrived.reshape(peers * BLOCK, width), whole_lambda, kept)
    returned = lax.all_to_all(values, "kblk", split_axis=0, concat_axis=0, tiled=True)
    return pick(matrix, returned)


def solution(mesh):
    placed = (P(("kblk", "amp"), None), P(("kblk", "amp"), None), P("kblk", "amp", None))
    return jax.shard_map(
        body, mesh=mesh, in_specs=placed, out_specs=P(("kblk", "amp"), None), check_vma=False
    )
```

```python
import jax
import jax.numpy as jnp
from jax import lax
from jax.experimental import pallas as pl
from jax.experimental.pallas import tpu as pltpu
from jax.sharding import PartitionSpec as P

CAP = 4
LARGEST = 32767.0
STEPS = 64
LANES = 128
BLOCK = 2 * CAP
PLACE_STEPS = 8
PLACE_AHEAD = 3
MULTIPLY_BLOCK = 1024
HEAD = 1536


def whole_in(space):
    return pl.BlockSpec(memory_space=space)


def slots_of(owner, upright=False):
    rows = owner.shape[1]
    across = jnp.broadcast_to(owner.astype(jnp.float32), (rows, rows))
    down = across.T
    first = lax.broadcasted_iota(jnp.int32, (rows, rows), 0)
    second = lax.broadcasted_iota(jnp.int32, (rows, rows), 1)
    if upright:
        earlier = jnp.where((across == down) & (second < first), 1, 0)
        return down[:, :1].astype(jnp.int32), jnp.sum(earlier, axis=1, keepdims=True)
    earlier = jnp.where((across == down) & (first < second), 1, 0)
    return jnp.sum(earlier, axis=0, keepdims=True)


def place_kernel(
    swap_ref, named_ref, integrals_ref, out_ref, owner_ref, both_ref, placed_ref, pick_ref, sem, named_sem
):
    rows, (lines, width) = integrals_ref.shape[0], out_ref.shape
    block = width // PLACE_STEPS

    def columns(i, half=0):
        return pl.ds(pl.multiple_of(half * width + i * block, block), block)

    def fetch(i, half):
        return pltpu.make_async_copy(
            integrals_ref.at[:, columns(i, half)],
            both_ref.at[pl.ds(half * rows, rows), columns(i)],
            sem.at[i, half],
        )

    def write(i):
        return pltpu.make_async_copy(
            placed_ref.at[:, columns(i)], out_ref.at[:, columns(i)], sem.at[i, 2]
        )

    names = pltpu.make_async_copy(named_ref, owner_ref, named_sem)
    names.start()
    for i in range(PLACE_AHEAD):
        fetch(i, 0).start()
        fetch(i, 1).start()

    names.wait()
    owner = owner_ref[...]
    line = owner * BLOCK + slots_of(owner)
    number = lax.broadcasted_iota(jnp.int32, (lines, rows), 0)
    swap = swap_ref[0] * CAP
    pick_ref[:, :rows] = jnp.where(number == line + swap, 1.0, 0.0).astype(jnp.bfloat16)
    pick_ref[:, rows:] = jnp.where(number == line + (CAP - swap), 1.0, 0.0).astype(jnp.bfloat16)

    @pl.loop(0, PLACE_STEPS)
    def _(i):
        @pl.when(i + PLACE_AHEAD < PLACE_STEPS)
        def _():
            fetch(i + PLACE_AHEAD, 0).start()
            fetch(i + PLACE_AHEAD, 1).start()

        fetch(i, 0).wait()
        fetch(i, 1).wait()
        placed_ref[:, columns(i)] = jnp.dot(
            pick_ref[...], both_ref[:, columns(i)], preferred_element_type=jnp.float32
        ).astype(jnp.bfloat16)
        write(i).start()

    @pl.loop(0, PLACE_STEPS)
    def _(i):
        write(i).wait()


def place(swap, owner, integrals, peers):
    rows, cols = integrals.shape
    lines, width = peers * BLOCK, cols // 2
    return pl.pallas_call(
        place_kernel,
        in_specs=[whole_in(pltpu.SMEM), whole_in(pl.ANY), whole_in(pl.ANY)],
        out_specs=whole_in(pl.ANY),
        out_shape=pltpu.HBM((lines, width), jnp.bfloat16),
        scratch_shapes=[
            pltpu.VMEM((1, rows), jnp.int32),
            pltpu.VMEM((2 * rows, width), jnp.bfloat16),
            pltpu.VMEM((lines, width), jnp.bfloat16),
            pltpu.VMEM((lines, 2 * rows), jnp.bfloat16),
            pltpu.SemaphoreType.DMA((PLACE_STEPS, 3)),
            pltpu.SemaphoreType.DMA,
        ],
        compiler_params=pltpu.CompilerParams(vmem_limit_bytes=24 * 1024 * 1024),
        cost_estimate=pl.CostEstimate(
            flops=4 * lines * rows * width,
            bytes_accessed=2 * (2 * rows + lines) * width,
            transcendentals=0,
        ),
        name="place",
    )(swap, *[pltpu.with_memory_space_constraint(x, pltpu.HBM) for x in (owner, integrals)])


def collect_kernel(
    amp_ref, owner_ref, mine_ref, left_ref, right_ref, top_ref, bottom_ref,
    out_ref, kept_ref, pick_ref, held_ref, sem,
):
    pairs = mine_ref.shape[0]
    count = out_ref.shape[0] // pairs
    shards = (
        (mine_ref, 0, 0),
        (left_ref, 1, 0),
        (right_ref, 3, 0),
        (top_ref, 2, 0),
        (bottom_ref, 2, pairs // 2),
    )
    fetches, writes = [], []
    for i, (ref, shift, skip) in enumerate(shards):
        at = (amp_ref[0] + count - shift) % count
        there = pl.ds(pl.multiple_of(at * pairs + skip, pairs // 2), ref.shape[0])
        fetches.append(pltpu.make_async_copy(ref, held_ref.at[there, :], sem.at[i, 0]))
        writes.append(
            pltpu.make_async_copy(held_ref.at[there, :], out_ref.at[there, :], sem.at[i, 1])
        )
    for copy in fetches:
        copy.start()
    owner, slot = slots_of(owner_ref[...], upright=True)
    lines = pick_ref.shape[1] // 2
    number = lax.broadcasted_iota(jnp.int32, (pick_ref.shape[0], lines), 1)
    here = jnp.where(number == owner * CAP + slot, 1.0, 0.0)
    pick_ref[:, :lines] = (here * 256.0).astype(jnp.bfloat16)
    pick_ref[:, lines:] = here.astype(jnp.bfloat16)
    for fetch, write in zip(fetches, writes):
        fetch.wait()
        write.start()
    kept, width = kept_ref.shape[1] // 2, out_ref.shape[1] // 2
    kept_ref[:, :kept] = held_ref[:, :kept]
    kept_ref[:, kept:] = held_ref[:, width : width + kept]
    for copy in writes:
        copy.wait()


def collect(amp, owner, shards, count, peers):
    pairs, cols = shards[0].shape
    kept = 2 * HEAD
    return pl.pallas_call(
        collect_kernel,
        in_specs=[whole_in(pltpu.SMEM), whole_in(pltpu.VMEM)] + [whole_in(pl.ANY)] * len(shards),
        out_specs=[whole_in(pl.ANY), whole_in(pltpu.VMEM), whole_in(pltpu.VMEM)],
        out_shape=[
            pltpu.HBM((count * pairs, cols), jnp.bfloat16),
            pltpu.VMEM((count * pairs, kept), jnp.bfloat16),
            jax.ShapeDtypeStruct((owner.shape[1], 2 * peers * CAP), jnp.bfloat16),
        ],
        scratch_shapes=[
            pltpu.VMEM((count * pairs, cols), jnp.bfloat16),
            pltpu.SemaphoreType.DMA((len(shards), 2)),
        ],
        compiler_params=pltpu.CompilerParams(vmem_limit_bytes=24 * 1024 * 1024),
        cost_estimate=pl.CostEstimate(
            flops=0, bytes_accessed=4 * count * pairs * cols, transcendentals=0
        ),
        name="collect",
    )(amp, owner, *[pltpu.with_memory_space_constraint(x, pltpu.HBM) for x in shards])


def exchange(x, group):
    lines = x.shape[0]
    return jnp.where(group == 0, pltpu.roll(x, lines - CAP, 0), pltpu.roll(x, CAP, 0))


def multiply_kernel(
    rows_ref, amps_ref, kept_ref, out_ref, near_ref, held_ref, low_ref, high_ref, sem
):
    lines, width = rows_ref.shape
    upper = lines // 2
    steps = (width - HEAD) // MULTIPLY_BLOCK
    tail = HEAD + steps * MULTIPLY_BLOCK

    def fetches(i, start, block, halves=2):
        at = [pl.ds(half * width + start, block) for half in range(2)]
        copies = [pltpu.make_async_copy(rows_ref.at[:, at[0]], near_ref.at[:, at[0]], sem.at[i, 0])]
        for half in range(halves):
            copies.append(
                pltpu.make_async_copy(
                    amps_ref.at[:, at[half]], held_ref.at[:, at[half]], sem.at[i, 1 + half]
                )
            )
        return copies

    def middle(i):
        start = pl.multiple_of(HEAD + i * MULTIPLY_BLOCK, 512)
        return fetches(1 + i, start, MULTIPLY_BLOCK), start

    def work(start, block, table_ref, half_width):
        group = lax.broadcasted_iota(jnp.int32, (upper, block), 0) // CAP % 2
        first, second = near_ref[:upper, pl.ds(start, block)], near_ref[upper:, pl.ds(start, block)]
        for half, total_ref in enumerate((low_ref, high_ref)):
            total_ref[...] += lax.dot_general(
                jnp.where(group == half, first, second),
                table_ref[:, pl.ds(half * half_width + start, block)],
                (((1,), (1,)), ((), ())),
                preferred_element_type=jnp.float32,
            )

    head = fetches(0, 0, HEAD, 0)[0]
    head.start()

    @pl.loop(0, steps)
    def _(i):
        for copy in middle(i)[0]:
            copy.start()

    rest = fetches(1 + steps, tail, width - tail)
    for copy in rest:
        copy.start()
    low_ref[...] = jnp.zeros_like(low_ref)
    high_ref[...] = jnp.zeros_like(high_ref)
    head.wait()
    work(0, HEAD, kept_ref, HEAD)

    @pl.loop(0, steps)
    def _(i):
        copies, start = middle(i)
        for copy in copies:
            copy.wait()
        work(start, MULTIPLY_BLOCK, held_ref, width)

    for copy in rest:
        copy.wait()
    work(tail, width - tail, held_ref, width)

    group = lax.broadcasted_iota(jnp.int32, low_ref.shape, 0) // CAP % 2
    value = low_ref[...] + exchange(high_ref[...], group)
    power = jnp.log2(jnp.maximum(jnp.max(jnp.abs(value), axis=1, keepdims=True), 2.0**-110))
    code = jnp.ceil(power * STEPS + 0.01).astype(jnp.int32)
    whole = jnp.round(value * (LARGEST / jnp.exp2(code.astype(jnp.float32) / STEPS)))
    whole = jnp.clip(whole, -LARGEST, LARGEST).astype(jnp.int32)
    whole = jnp.concatenate([whole, jnp.broadcast_to(code, (upper, LANES))], axis=1)
    blocks = whole.reshape(upper // BLOCK, 2, CAP, whole.shape[1])
    for j in range(2):
        first = j * (upper // BLOCK)
        out_ref[first : first + upper // BLOCK] = blocks[:, j].astype(jnp.int16)


def multiply(rows, amps, kept):
    lines, width = rows.shape
    pairs = amps.shape[0]
    return pl.pallas_call(
        multiply_kernel,
        in_specs=[whole_in(pl.ANY), whole_in(pl.ANY), whole_in(pltpu.VMEM)],
        out_specs=whole_in(pltpu.VMEM),
        out_shape=jax.ShapeDtypeStruct((lines // BLOCK, CAP, pairs + LANES), jnp.int16),
        scratch_shapes=[
            pltpu.VMEM((lines, width), jnp.bfloat16),
            pltpu.VMEM((pairs, 2 * width), jnp.bfloat16),
            pltpu.VMEM((lines // 2, pairs), jnp.float32),
            pltpu.VMEM((lines // 2, pairs), jnp.float32),
            pltpu.SemaphoreType.DMA((2 + (width - HEAD) // MULTIPLY_BLOCK, 3)),
        ],
        compiler_params=pltpu.CompilerParams(vmem_limit_bytes=40 * 1024 * 1024),
        cost_estimate=pl.CostEstimate(
            flops=2 * lines * pairs * width,
            bytes_accessed=2 * (lines + 2 * pairs) * width,
            transcendentals=0,
        ),
        name="multiply",
    )(
        pltpu.with_memory_space_constraint(rows, pltpu.HBM),
        pltpu.with_memory_space_constraint(amps, pltpu.HBM),
        pltpu.with_memory_space_constraint(kept, pltpu.VMEM),
    )


def pick_kernel(pick_ref, lines_ref, out_ref):
    lines, pairs = pick_ref.shape[1] // 2, out_ref.shape[1]
    whole = lines_ref[...].astype(jnp.int32).reshape(lines, lines_ref.shape[2])
    upper = whole >> 8
    parts = jnp.concatenate([upper, whole - (upper << 8)], axis=0)
    picked = jnp.dot(
        pick_ref[...],
        parts.astype(jnp.float32).astype(jnp.bfloat16),
        preferred_element_type=jnp.float32,
    )
    unit = jnp.exp2(picked[:, pairs : pairs + 1] / STEPS) / LARGEST
    out_ref[...] = picked[:, :pairs] * unit


def pick(matrix, lines):
    rows, pairs = matrix.shape[0], lines.shape[2] - LANES
    return pl.pallas_call(
        pick_kernel,
        in_specs=[whole_in(pltpu.VMEM)] * 2,
        out_specs=whole_in(pltpu.VMEM),
        out_shape=jax.ShapeDtypeStruct((rows, pairs), jnp.float32),
        cost_estimate=pl.CostEstimate(
            flops=4 * rows * lines.size,
            bytes_accessed=2 * lines.size + 4 * rows * pairs,
            transcendentals=rows,
        ),
        name="pick",
    )(matrix, pltpu.with_memory_space_constraint(lines, pltpu.VMEM))


def body(integrals, row_owner, lambda_amps):
    peers, amps = lax.axis_size("kblk"), lax.axis_size("amp")
    amp = lax.axis_index("amp").astype(jnp.int32)
    swap = (lax.axis_index("kblk") >= peers // 2).astype(jnp.int32)
    mine = lambda_amps[0]
    middle = mine.shape[0] // 2
    ahead = [(i, (i + 1) % amps) for i in range(amps)]
    back = [(i, (i - 1) % amps) for i in range(amps)]
    left, right = lax.ppermute(mine, "amp", ahead), lax.ppermute(mine, "amp", back)
    top = lax.ppermute(left[:middle], "amp", ahead)
    bottom = lax.ppermute(right[middle:], "amp", back)
    owner = row_owner.reshape(1, -1)
    whole_lambda, kept, matrix = collect(
        amp[None], owner, (mine, left, right, top, bottom), amps, peers
    )

    placed = place(swap[None], owner, integrals, peers)
    width = placed.shape[1]
    arrived = lax.all_to_all(
        placed.reshape(peers, BLOCK, width), "kblk", split_axis=0, concat_axis=0, tiled=True
    )
    values = multiply(arrived.reshape(peers * BLOCK, width), whole_lambda, kept)
    returned = lax.all_to_all(values, "kblk", split_axis=0, concat_axis=0, tiled=True)
    return pick(matrix, returned)


def solution(mesh):
    placed = (P(("kblk", "amp"), None), P(("kblk", "amp"), None), P("kblk", "amp", None))
    return jax.shard_map(
        body, mesh=mesh, in_specs=placed, out_specs=P(("kblk", "amp"), None), check_vma=False
    )
```

```python
import jax
import jax.numpy as jnp
from jax import lax
from jax.experimental import pallas as pl
from jax.experimental.pallas import tpu as pltpu
from jax.sharding import PartitionSpec as P

CAP = 4
LARGEST = 32767.0
STEPS = 64
LANES = 128
BLOCK = 2 * CAP
PLACE_STEPS = 8
MULTIPLY_BLOCK = 1024
HEAD = 1536


def whole_in(space):
    return pl.BlockSpec(memory_space=space)


def slots_of(owner, upright=False):
    rows = owner.shape[1]
    across = jnp.broadcast_to(owner.astype(jnp.float32), (rows, rows))
    down = across.T
    first = lax.broadcasted_iota(jnp.int32, (rows, rows), 0)
    second = lax.broadcasted_iota(jnp.int32, (rows, rows), 1)
    if upright:
        earlier = jnp.where((across == down) & (second < first), 1, 0)
        return down[:, :1].astype(jnp.int32), jnp.sum(earlier, axis=1, keepdims=True)
    earlier = jnp.where((across == down) & (first < second), 1, 0)
    return jnp.sum(earlier, axis=0, keepdims=True)


def place_kernel(swap_ref, owner_ref, integrals_ref, out_ref, both_ref, placed_ref, pick_ref, sem):
    rows, (lines, width) = integrals_ref.shape[0], out_ref.shape
    block = width // PLACE_STEPS

    def columns(i, half=0):
        return pl.ds(pl.multiple_of(half * width + i * block, block), block)

    def fetch(i, half):
        return pltpu.make_async_copy(
            integrals_ref.at[:, columns(i, half)],
            both_ref.at[pl.ds(half * rows, rows), columns(i)],
            sem.at[i, half],
        )

    def write(i):
        return pltpu.make_async_copy(
            placed_ref.at[:, columns(i)], out_ref.at[:, columns(i)], sem.at[i, 2]
        )

    @pl.loop(0, PLACE_STEPS)
    def _(i):
        fetch(i, 0).start()
        fetch(i, 1).start()

    owner = owner_ref[...]
    line = owner * BLOCK + slots_of(owner)
    number = lax.broadcasted_iota(jnp.int32, (lines, rows), 0)
    swap = swap_ref[0] * CAP
    pick_ref[:, :rows] = jnp.where(number == line + swap, 1.0, 0.0).astype(jnp.bfloat16)
    pick_ref[:, rows:] = jnp.where(number == line + (CAP - swap), 1.0, 0.0).astype(jnp.bfloat16)

    @pl.loop(0, PLACE_STEPS)
    def _(i):
        fetch(i, 0).wait()
        fetch(i, 1).wait()
        placed_ref[:, columns(i)] = jnp.dot(
            pick_ref[...], both_ref[:, columns(i)], preferred_element_type=jnp.float32
        ).astype(jnp.bfloat16)
        write(i).start()

    @pl.loop(0, PLACE_STEPS)
    def _(i):
        write(i).wait()


def place(swap, owner, integrals, peers):
    rows, cols = integrals.shape
    lines, width = peers * BLOCK, cols // 2
    return pl.pallas_call(
        place_kernel,
        in_specs=[whole_in(pltpu.SMEM), whole_in(pltpu.VMEM), whole_in(pl.ANY)],
        out_specs=whole_in(pl.ANY),
        out_shape=pltpu.HBM((lines, width), jnp.bfloat16),
        scratch_shapes=[
            pltpu.VMEM((2 * rows, width), jnp.bfloat16),
            pltpu.VMEM((lines, width), jnp.bfloat16),
            pltpu.VMEM((lines, 2 * rows), jnp.bfloat16),
            pltpu.SemaphoreType.DMA((PLACE_STEPS, 3)),
        ],
        compiler_params=pltpu.CompilerParams(vmem_limit_bytes=24 * 1024 * 1024),
        cost_estimate=pl.CostEstimate(
            flops=4 * lines * rows * width,
            bytes_accessed=2 * (2 * rows + lines) * width,
            transcendentals=0,
        ),
        name="place",
    )(swap, owner, pltpu.with_memory_space_constraint(integrals, pltpu.HBM))


def collect_kernel(
    amp_ref, owner_ref, mine_ref, left_ref, right_ref, top_ref, bottom_ref,
    out_ref, kept_ref, pick_ref, held_ref, sem,
):
    pairs = mine_ref.shape[0]
    count = out_ref.shape[0] // pairs
    shards = (
        (mine_ref, 0, 0),
        (left_ref, 1, 0),
        (right_ref, 3, 0),
        (top_ref, 2, 0),
        (bottom_ref, 2, pairs // 2),
    )
    fetches, writes = [], []
    for i, (ref, shift, skip) in enumerate(shards):
        at = (amp_ref[0] + count - shift) % count
        there = pl.ds(pl.multiple_of(at * pairs + skip, pairs // 2), ref.shape[0])
        fetches.append(pltpu.make_async_copy(ref, held_ref.at[there, :], sem.at[i, 0]))
        writes.append(
            pltpu.make_async_copy(held_ref.at[there, :], out_ref.at[there, :], sem.at[i, 1])
        )
    for copy in fetches:
        copy.start()
    owner, slot = slots_of(owner_ref[...], upright=True)
    lines = pick_ref.shape[1] // 2
    number = lax.broadcasted_iota(jnp.int32, (pick_ref.shape[0], lines), 1)
    here = jnp.where(number == owner * CAP + slot, 1.0, 0.0)
    pick_ref[:, :lines] = (here * 256.0).astype(jnp.bfloat16)
    pick_ref[:, lines:] = here.astype(jnp.bfloat16)
    for fetch, write in zip(fetches, writes):
        fetch.wait()
        write.start()
    kept, width = kept_ref.shape[1] // 2, out_ref.shape[1] // 2
    kept_ref[:, :kept] = held_ref[:, :kept]
    kept_ref[:, kept:] = held_ref[:, width : width + kept]
    for copy in writes:
        copy.wait()


def collect(amp, owner, shards, count, peers):
    pairs, cols = shards[0].shape
    kept = 2 * HEAD
    return pl.pallas_call(
        collect_kernel,
        in_specs=[whole_in(pltpu.SMEM), whole_in(pltpu.VMEM)] + [whole_in(pl.ANY)] * len(shards),
        out_specs=[whole_in(pl.ANY), whole_in(pltpu.VMEM), whole_in(pltpu.VMEM)],
        out_shape=[
            pltpu.HBM((count * pairs, cols), jnp.bfloat16),
            pltpu.VMEM((count * pairs, kept), jnp.bfloat16),
            jax.ShapeDtypeStruct((owner.shape[1], 2 * peers * CAP), jnp.bfloat16),
        ],
        scratch_shapes=[
            pltpu.VMEM((count * pairs, cols), jnp.bfloat16),
            pltpu.SemaphoreType.DMA((len(shards), 2)),
        ],
        compiler_params=pltpu.CompilerParams(vmem_limit_bytes=24 * 1024 * 1024),
        cost_estimate=pl.CostEstimate(
            flops=0, bytes_accessed=4 * count * pairs * cols, transcendentals=0
        ),
        name="collect",
    )(amp, owner, *[pltpu.with_memory_space_constraint(x, pltpu.HBM) for x in shards])


def exchange(x, group):
    lines = x.shape[0]
    return jnp.where(group == 0, pltpu.roll(x, lines - CAP, 0), pltpu.roll(x, CAP, 0))


def multiply_kernel(
    rows_ref, amps_ref, kept_ref, out_ref, near_ref, held_ref, low_ref, high_ref, sem
):
    lines, width = rows_ref.shape
    upper = lines // 2
    steps = (width - HEAD) // MULTIPLY_BLOCK
    tail = HEAD + steps * MULTIPLY_BLOCK

    def fetches(i, start, block, halves=2):
        at = [pl.ds(half * width + start, block) for half in range(2)]
        copies = [pltpu.make_async_copy(rows_ref.at[:, at[0]], near_ref.at[:, at[0]], sem.at[i, 0])]
        for half in range(halves):
            copies.append(
                pltpu.make_async_copy(
                    amps_ref.at[:, at[half]], held_ref.at[:, at[half]], sem.at[i, 1 + half]
                )
            )
        return copies

    def middle(i):
        start = pl.multiple_of(HEAD + i * MULTIPLY_BLOCK, 512)
        return fetches(1 + i, start, MULTIPLY_BLOCK), start

    def work(start, block, table_ref, half_width):
        group = lax.broadcasted_iota(jnp.int32, (upper, block), 0) // CAP % 2
        first, second = near_ref[:upper, pl.ds(start, block)], near_ref[upper:, pl.ds(start, block)]
        for half, total_ref in enumerate((low_ref, high_ref)):
            total_ref[...] += lax.dot_general(
                jnp.where(group == half, first, second),
                table_ref[:, pl.ds(half * half_width + start, block)],
                (((1,), (1,)), ((), ())),
                preferred_element_type=jnp.float32,
            )

    head = fetches(0, 0, HEAD, 0)[0]
    head.start()

    @pl.loop(0, steps)
    def _(i):
        for copy in middle(i)[0]:
            copy.start()

    rest = fetches(1 + steps, tail, width - tail)
    for copy in rest:
        copy.start()
    low_ref[...] = jnp.zeros_like(low_ref)
    high_ref[...] = jnp.zeros_like(high_ref)
    head.wait()
    work(0, HEAD, kept_ref, HEAD)

    @pl.loop(0, steps)
    def _(i):
        copies, start = middle(i)
        for copy in copies:
            copy.wait()
        work(start, MULTIPLY_BLOCK, held_ref, width)

    for copy in rest:
        copy.wait()
    work(tail, width - tail, held_ref, width)

    group = lax.broadcasted_iota(jnp.int32, low_ref.shape, 0) // CAP % 2
    value = low_ref[...] + exchange(high_ref[...], group)
    power = jnp.log2(jnp.maximum(jnp.max(jnp.abs(value), axis=1, keepdims=True), 2.0**-110))
    code = jnp.ceil(power * STEPS + 0.01).astype(jnp.int32)
    whole = jnp.round(value * (LARGEST / jnp.exp2(code.astype(jnp.float32) / STEPS)))
    whole = jnp.clip(whole, -LARGEST, LARGEST).astype(jnp.int32)
    whole = jnp.concatenate([whole, jnp.broadcast_to(code, (upper, LANES))], axis=1)
    blocks = whole.reshape(upper // BLOCK, 2, CAP, whole.shape[1])
    for j in range(2):
        first = j * (upper // BLOCK)
        out_ref[first : first + upper // BLOCK] = blocks[:, j].astype(jnp.int16)


def multiply(rows, amps, kept):
    lines, width = rows.shape
    pairs = amps.shape[0]
    return pl.pallas_call(
        multiply_kernel,
        in_specs=[whole_in(pl.ANY), whole_in(pl.ANY), whole_in(pltpu.VMEM)],
        out_specs=whole_in(pltpu.VMEM),
        out_shape=pltpu.VMEM((lines // BLOCK, CAP, pairs + LANES), jnp.int16),
        scratch_shapes=[
            pltpu.VMEM((lines, width), jnp.bfloat16),
            pltpu.VMEM((pairs, 2 * width), jnp.bfloat16),
            pltpu.VMEM((lines // 2, pairs), jnp.float32),
            pltpu.VMEM((lines // 2, pairs), jnp.float32),
            pltpu.SemaphoreType.DMA((2 + (width - HEAD) // MULTIPLY_BLOCK, 3)),
        ],
        compiler_params=pltpu.CompilerParams(vmem_limit_bytes=40 * 1024 * 1024),
        cost_estimate=pl.CostEstimate(
            flops=2 * lines * pairs * width,
            bytes_accessed=2 * (lines + 2 * pairs) * width,
            transcendentals=0,
        ),
        name="multiply",
    )(
        pltpu.with_memory_space_constraint(rows, pltpu.HBM),
        pltpu.with_memory_space_constraint(amps, pltpu.HBM),
        pltpu.with_memory_space_constraint(kept, pltpu.VMEM),
    )


def pick_kernel(matrix_ref, lines_ref, out_ref, pick_ref, parts_ref, held_ref, sem):
    lines, pairs = pick_ref.shape[1] // 2, out_ref.shape[1]
    fetch = pltpu.make_async_copy(matrix_ref, pick_ref, sem.at[0])
    fetch.start()
    whole = lines_ref[...].astype(jnp.int32).reshape(lines, lines_ref.shape[2])
    upper = whole >> 8
    parts_ref[:lines, :] = upper.astype(jnp.float32).astype(jnp.bfloat16)
    parts_ref[lines:, :] = (whole - (upper << 8)).astype(jnp.float32).astype(jnp.bfloat16)
    fetch.wait()

    def picked(first, count):
        return jnp.dot(
            pick_ref[...],
            parts_ref[:, first : first + count],
            preferred_element_type=jnp.float32,
        )

    unit = jnp.exp2(picked(pairs, LANES)[:, :1] / STEPS) / LARGEST
    writes = []
    for i in range(2):
        first, count = i * (pairs // 2), pairs // 2
        held_ref[:, first : first + count] = picked(first, count) * unit
        here = pl.ds(first, count)
        writes.append(pltpu.make_async_copy(held_ref.at[:, here], out_ref.at[:, here], sem.at[1 + i]))
        writes[-1].start()
    for write in writes:
        write.wait()


def pick(matrix, lines):
    rows, pairs = matrix.shape[0], lines.shape[2] - LANES
    return pl.pallas_call(
        pick_kernel,
        in_specs=[whole_in(pl.ANY), whole_in(pltpu.VMEM)],
        out_specs=whole_in(pl.ANY),
        out_shape=jax.ShapeDtypeStruct((rows, pairs), jnp.float32),
        scratch_shapes=[
            pltpu.VMEM(matrix.shape, jnp.bfloat16),
            pltpu.VMEM((matrix.shape[1], lines.shape[2]), jnp.bfloat16),
            pltpu.VMEM((rows, pairs), jnp.float32),
            pltpu.SemaphoreType.DMA((3,)),
        ],
        cost_estimate=pl.CostEstimate(
            flops=4 * rows * lines.size,
            bytes_accessed=2 * lines.size + 4 * rows * pairs,
            transcendentals=rows,
        ),
        name="pick",
    )(
        pltpu.with_memory_space_constraint(matrix, pltpu.HBM),
        pltpu.with_memory_space_constraint(lines, pltpu.VMEM),
    )


def body(integrals, row_owner, lambda_amps):
    peers, amps = lax.axis_size("kblk"), lax.axis_size("amp")
    amp = lax.axis_index("amp").astype(jnp.int32)
    swap = (lax.axis_index("kblk") >= peers // 2).astype(jnp.int32)
    mine = lambda_amps[0]
    middle = mine.shape[0] // 2
    ahead = [(i, (i + 1) % amps) for i in range(amps)]
    back = [(i, (i - 1) % amps) for i in range(amps)]
    left, right = lax.ppermute(mine, "amp", ahead), lax.ppermute(mine, "amp", back)
    top = lax.ppermute(left[:middle], "amp", ahead)
    bottom = lax.ppermute(right[middle:], "amp", back)
    owner = row_owner.reshape(1, -1)
    whole_lambda, kept, matrix = collect(
        amp[None], owner, (mine, left, right, top, bottom), amps, peers
    )

    placed = place(swap[None], owner, integrals, peers)
    width = placed.shape[1]
    arrived = lax.all_to_all(
        placed.reshape(peers, BLOCK, width), "kblk", split_axis=0, concat_axis=0, tiled=True
    )
    values = multiply(arrived.reshape(peers * BLOCK, width), whole_lambda, kept)
    returned = lax.all_to_all(values, "kblk", split_axis=0, concat_axis=0, tiled=True)
    return pick(matrix, returned)


def solution(mesh):
    placed = (P(("kblk", "amp"), None), P(("kblk", "amp"), None), P("kblk", "amp", None))
    return jax.shard_map(
        body, mesh=mesh, in_specs=placed, out_specs=P(("kblk", "amp"), None), check_vma=False
    )
```

```python
import jax
import jax.numpy as jnp
from jax import lax
from jax.experimental import pallas as pl
from jax.experimental.pallas import tpu as pltpu
from jax.sharding import PartitionSpec as P

CAP = 4
LARGEST = 32767.0
STEPS = 64
LANES = 128
BLOCK = 2 * CAP
PLACE_BLOCKS = (1024, 2048, 2048, 2048, 1024)
MULTIPLY_BLOCK = 1024
HEAD = 1536


def whole_in(space):
    return pl.BlockSpec(memory_space=space)


def slots_of(owner, upright=False):
    rows = owner.shape[1]
    across = jnp.broadcast_to(owner.astype(jnp.float32), (rows, rows))
    down = across.T
    first = lax.broadcasted_iota(jnp.int32, (rows, rows), 0)
    second = lax.broadcasted_iota(jnp.int32, (rows, rows), 1)
    if upright:
        earlier = jnp.where((across == down) & (second < first), 1, 0)
        return down[:, :1].astype(jnp.int32), jnp.sum(earlier, axis=1, keepdims=True)
    earlier = jnp.where((across == down) & (first < second), 1, 0)
    return jnp.sum(earlier, axis=0, keepdims=True)


def place_kernel(swap_ref, owner_ref, integrals_ref, out_ref, both_ref, placed_ref, pick_ref, sem):
    rows, (lines, width) = integrals_ref.shape[0], out_ref.shape
    starts = [sum(PLACE_BLOCKS[:i]) for i in range(len(PLACE_BLOCKS))]

    def fetch(i, half):
        start, block = starts[i], PLACE_BLOCKS[i]
        return pltpu.make_async_copy(
            integrals_ref.at[:, pl.ds(half * width + start, block)],
            both_ref.at[pl.ds(half * rows, rows), pl.ds(start, block)],
            sem.at[i, half],
        )

    fetches = [[fetch(i, half) for half in range(2)] for i in range(len(PLACE_BLOCKS))]
    for pair in fetches:
        for copy in pair:
            copy.start()

    owner = owner_ref[...]
    line = owner * BLOCK + slots_of(owner)
    number = lax.broadcasted_iota(jnp.int32, (lines, rows), 0)
    swap = swap_ref[0] * CAP
    pick_ref[:, :rows] = jnp.where(number == line + swap, 1.0, 0.0).astype(jnp.bfloat16)
    pick_ref[:, rows:] = jnp.where(number == line + (CAP - swap), 1.0, 0.0).astype(jnp.bfloat16)

    writes = []
    for i, pair in enumerate(fetches):
        for copy in pair:
            copy.wait()
        here = pl.ds(starts[i], PLACE_BLOCKS[i])
        placed_ref[:, here] = jnp.dot(
            pick_ref[...], both_ref[:, here], preferred_element_type=jnp.float32
        ).astype(jnp.bfloat16)
        writes.append(pltpu.make_async_copy(placed_ref.at[:, here], out_ref.at[:, here], sem.at[i, 2]))
        writes[-1].start()
    for write in writes:
        write.wait()


def place(swap, owner, integrals, peers):
    rows, cols = integrals.shape
    lines, width = peers * BLOCK, cols // 2
    return pl.pallas_call(
        place_kernel,
        in_specs=[whole_in(pltpu.SMEM), whole_in(pltpu.VMEM), whole_in(pl.ANY)],
        out_specs=whole_in(pl.ANY),
        out_shape=pltpu.HBM((lines, width), jnp.bfloat16),
        scratch_shapes=[
            pltpu.VMEM((2 * rows, width), jnp.bfloat16),
            pltpu.VMEM((lines, width), jnp.bfloat16),
            pltpu.VMEM((lines, 2 * rows), jnp.bfloat16),
            pltpu.SemaphoreType.DMA((len(PLACE_BLOCKS), 3)),
        ],
        compiler_params=pltpu.CompilerParams(vmem_limit_bytes=24 * 1024 * 1024),
        cost_estimate=pl.CostEstimate(
            flops=4 * lines * rows * width,
            bytes_accessed=2 * (2 * rows + lines) * width,
            transcendentals=0,
        ),
        name="place",
    )(swap, owner, pltpu.with_memory_space_constraint(integrals, pltpu.HBM))


def collect_kernel(
    amp_ref, owner_ref, mine_ref, left_ref, right_ref, top_ref, bottom_ref,
    out_ref, kept_ref, pick_ref, held_ref, sem,
):
    pairs = mine_ref.shape[0]
    count = out_ref.shape[0] // pairs
    shards = (
        (mine_ref, 0, 0),
        (left_ref, 1, 0),
        (right_ref, 3, 0),
        (top_ref, 2, 0),
        (bottom_ref, 2, pairs // 2),
    )
    fetches, writes = [], []
    for i, (ref, shift, skip) in enumerate(shards):
        at = (amp_ref[0] + count - shift) % count
        there = pl.ds(pl.multiple_of(at * pairs + skip, pairs // 2), ref.shape[0])
        fetches.append(pltpu.make_async_copy(ref, held_ref.at[there, :], sem.at[i, 0]))
        writes.append(
            pltpu.make_async_copy(held_ref.at[there, :], out_ref.at[there, :], sem.at[i, 1])
        )
    for copy in fetches:
        copy.start()
    owner, slot = slots_of(owner_ref[...], upright=True)
    lines = pick_ref.shape[1] // 2
    number = lax.broadcasted_iota(jnp.int32, (pick_ref.shape[0], lines), 1)
    here = jnp.where(number == owner * CAP + slot, 1.0, 0.0)
    pick_ref[:, :lines] = (here * 256.0).astype(jnp.bfloat16)
    pick_ref[:, lines:] = here.astype(jnp.bfloat16)
    for fetch, write in zip(fetches, writes):
        fetch.wait()
        write.start()
    kept, width = kept_ref.shape[1] // 2, out_ref.shape[1] // 2
    kept_ref[:, :kept] = held_ref[:, :kept]
    kept_ref[:, kept:] = held_ref[:, width : width + kept]
    for copy in writes:
        copy.wait()


def collect(amp, owner, shards, count, peers):
    pairs, cols = shards[0].shape
    kept = 2 * HEAD
    return pl.pallas_call(
        collect_kernel,
        in_specs=[whole_in(pltpu.SMEM), whole_in(pltpu.VMEM)] + [whole_in(pl.ANY)] * len(shards),
        out_specs=[whole_in(pl.ANY), whole_in(pltpu.VMEM), whole_in(pltpu.VMEM)],
        out_shape=[
            pltpu.HBM((count * pairs, cols), jnp.bfloat16),
            pltpu.VMEM((count * pairs, kept), jnp.bfloat16),
            jax.ShapeDtypeStruct((owner.shape[1], 2 * peers * CAP), jnp.bfloat16),
        ],
        scratch_shapes=[
            pltpu.VMEM((count * pairs, cols), jnp.bfloat16),
            pltpu.SemaphoreType.DMA((len(shards), 2)),
        ],
        compiler_params=pltpu.CompilerParams(vmem_limit_bytes=24 * 1024 * 1024),
        cost_estimate=pl.CostEstimate(
            flops=0, bytes_accessed=4 * count * pairs * cols, transcendentals=0
        ),
        name="collect",
    )(amp, owner, *[pltpu.with_memory_space_constraint(x, pltpu.HBM) for x in shards])


def exchange(x, group):
    lines = x.shape[0]
    return jnp.where(group == 0, pltpu.roll(x, lines - CAP, 0), pltpu.roll(x, CAP, 0))


def multiply_kernel(
    rows_ref, amps_ref, kept_ref, out_ref, near_ref, held_ref, low_ref, high_ref, sem
):
    lines, width = rows_ref.shape
    upper = lines // 2
    steps = (width - HEAD) // MULTIPLY_BLOCK
    tail = HEAD + steps * MULTIPLY_BLOCK

    def fetches(i, start, block, halves=2):
        at = [pl.ds(half * width + start, block) for half in range(2)]
        copies = [pltpu.make_async_copy(rows_ref.at[:, at[0]], near_ref.at[:, at[0]], sem.at[i, 0])]
        for half in range(halves):
            copies.append(
                pltpu.make_async_copy(
                    amps_ref.at[:, at[half]], held_ref.at[:, at[half]], sem.at[i, 1 + half]
                )
            )
        return copies

    def middle(i):
        start = pl.multiple_of(HEAD + i * MULTIPLY_BLOCK, 512)
        return fetches(1 + i, start, MULTIPLY_BLOCK), start

    def work(start, block, table_ref, half_width):
        group = lax.broadcasted_iota(jnp.int32, (upper, block), 0) // CAP % 2
        first, second = near_ref[:upper, pl.ds(start, block)], near_ref[upper:, pl.ds(start, block)]
        for half, total_ref in enumerate((low_ref, high_ref)):
            total_ref[...] += lax.dot_general(
                jnp.where(group == half, first, second),
                table_ref[:, pl.ds(half * half_width + start, block)],
                (((1,), (1,)), ((), ())),
                preferred_element_type=jnp.float32,
            )

    head = fetches(0, 0, HEAD, 0)[0]
    head.start()

    @pl.loop(0, steps)
    def _(i):
        for copy in middle(i)[0]:
            copy.start()

    rest = fetches(1 + steps, tail, width - tail)
    for copy in rest:
        copy.start()
    low_ref[...] = jnp.zeros_like(low_ref)
    high_ref[...] = jnp.zeros_like(high_ref)
    head.wait()
    work(0, HEAD, kept_ref, HEAD)

    @pl.loop(0, steps)
    def _(i):
        copies, start = middle(i)
        for copy in copies:
            copy.wait()
        work(start, MULTIPLY_BLOCK, held_ref, width)

    for copy in rest:
        copy.wait()
    work(tail, width - tail, held_ref, width)

    group = lax.broadcasted_iota(jnp.int32, low_ref.shape, 0) // CAP % 2
    value = low_ref[...] + exchange(high_ref[...], group)
    power = jnp.log2(jnp.maximum(jnp.max(jnp.abs(value), axis=1, keepdims=True), 2.0**-110))
    code = jnp.ceil(power * STEPS + 0.01).astype(jnp.int32)
    whole = jnp.round(value * (LARGEST / jnp.exp2(code.astype(jnp.float32) / STEPS)))
    whole = jnp.clip(whole, -LARGEST, LARGEST).astype(jnp.int32)
    whole = jnp.concatenate([whole, jnp.broadcast_to(code, (upper, LANES))], axis=1)
    blocks = whole.reshape(upper // BLOCK, 2, CAP, whole.shape[1])
    for j in range(2):
        first = j * (upper // BLOCK)
        out_ref[first : first + upper // BLOCK] = blocks[:, j].astype(jnp.int16)


def multiply(rows, amps, kept):
    lines, width = rows.shape
    pairs = amps.shape[0]
    return pl.pallas_call(
        multiply_kernel,
        in_specs=[whole_in(pl.ANY), whole_in(pl.ANY), whole_in(pltpu.VMEM)],
        out_specs=whole_in(pltpu.VMEM),
        out_shape=pltpu.VMEM((lines // BLOCK, CAP, pairs + LANES), jnp.int16),
        scratch_shapes=[
            pltpu.VMEM((lines, width), jnp.bfloat16),
            pltpu.VMEM((pairs, 2 * width), jnp.bfloat16),
            pltpu.VMEM((lines // 2, pairs), jnp.float32),
            pltpu.VMEM((lines // 2, pairs), jnp.float32),
            pltpu.SemaphoreType.DMA((2 + (width - HEAD) // MULTIPLY_BLOCK, 3)),
        ],
        compiler_params=pltpu.CompilerParams(vmem_limit_bytes=40 * 1024 * 1024),
        cost_estimate=pl.CostEstimate(
            flops=2 * lines * pairs * width,
            bytes_accessed=2 * (lines + 2 * pairs) * width,
            transcendentals=0,
        ),
        name="multiply",
    )(
        pltpu.with_memory_space_constraint(rows, pltpu.HBM),
        pltpu.with_memory_space_constraint(amps, pltpu.HBM),
        pltpu.with_memory_space_constraint(kept, pltpu.VMEM),
    )


def pick_kernel(matrix_ref, lines_ref, out_ref, pick_ref, parts_ref, held_ref, sem):
    lines, pairs = pick_ref.shape[1] // 2, out_ref.shape[1]
    fetch = pltpu.make_async_copy(matrix_ref, pick_ref, sem.at[0])
    fetch.start()
    whole = lines_ref[...].astype(jnp.int32).reshape(lines, lines_ref.shape[2])
    upper = whole >> 8
    parts_ref[:lines, :] = upper.astype(jnp.float32).astype(jnp.bfloat16)
    parts_ref[lines:, :] = (whole - (upper << 8)).astype(jnp.float32).astype(jnp.bfloat16)
    fetch.wait()

    def picked(first, count):
        return jnp.dot(
            pick_ref[...],
            parts_ref[:, first : first + count],
            preferred_element_type=jnp.float32,
        )

    unit = jnp.exp2(picked(pairs, LANES)[:, :1] / STEPS) / LARGEST
    writes = []
    for i in range(2):
        first, count = i * (pairs // 2), pairs // 2
        held_ref[:, first : first + count] = picked(first, count) * unit
        here = pl.ds(first, count)
        writes.append(pltpu.make_async_copy(held_ref.at[:, here], out_ref.at[:, here], sem.at[1 + i]))
        writes[-1].start()
    for write in writes:
        write.wait()


def pick(matrix, lines):
    rows, pairs = matrix.shape[0], lines.shape[2] - LANES
    return pl.pallas_call(
        pick_kernel,
        in_specs=[whole_in(pl.ANY), whole_in(pltpu.VMEM)],
        out_specs=whole_in(pl.ANY),
        out_shape=jax.ShapeDtypeStruct((rows, pairs), jnp.float32),
        scratch_shapes=[
            pltpu.VMEM(matrix.shape, jnp.bfloat16),
            pltpu.VMEM((matrix.shape[1], lines.shape[2]), jnp.bfloat16),
            pltpu.VMEM((rows, pairs), jnp.float32),
            pltpu.SemaphoreType.DMA((3,)),
        ],
        cost_estimate=pl.CostEstimate(
            flops=4 * rows * lines.size,
            bytes_accessed=2 * lines.size + 4 * rows * pairs,
            transcendentals=rows,
        ),
        name="pick",
    )(
        pltpu.with_memory_space_constraint(matrix, pltpu.HBM),
        pltpu.with_memory_space_constraint(lines, pltpu.VMEM),
    )


def body(integrals, row_owner, lambda_amps):
    peers, amps = lax.axis_size("kblk"), lax.axis_size("amp")
    amp = lax.axis_index("amp").astype(jnp.int32)
    swap = (lax.axis_index("kblk") >= peers // 2).astype(jnp.int32)
    mine = lambda_amps[0]
    middle = mine.shape[0] // 2
    ahead = [(i, (i + 1) % amps) for i in range(amps)]
    back = [(i, (i - 1) % amps) for i in range(amps)]
    left, right = lax.ppermute(mine, "amp", ahead), lax.ppermute(mine, "amp", back)
    top = lax.ppermute(left[:middle], "amp", ahead)
    bottom = lax.ppermute(right[middle:], "amp", back)
    owner = row_owner.reshape(1, -1)
    whole_lambda, kept, matrix = collect(
        amp[None], owner, (mine, left, right, top, bottom), amps, peers
    )

    placed = place(swap[None], owner, integrals, peers)
    width = placed.shape[1]
    arrived = lax.all_to_all(
        placed.reshape(peers, BLOCK, width), "kblk", split_axis=0, concat_axis=0, tiled=True
    )
    values = multiply(arrived.reshape(peers * BLOCK, width), whole_lambda, kept)
    returned = lax.all_to_all(values, "kblk", split_axis=0, concat_axis=0, tiled=True)
    return pick(matrix, returned)


def solution(mesh):
    placed = (P(("kblk", "amp"), None), P(("kblk", "amp"), None), P("kblk", "amp", None))
    return jax.shard_map(
        body, mesh=mesh, in_specs=placed, out_specs=P(("kblk", "amp"), None), check_vma=False
    )
```

```python
import jax
import jax.numpy as jnp
from jax import lax
from jax.experimental import pallas as pl
from jax.experimental.pallas import tpu as pltpu
from jax.sharding import PartitionSpec as P

CAP = 4
LARGEST = 32767.0
STEPS = 64
LANES = 128
BLOCK = 2 * CAP
PLACE_BLOCKS = (1024, 2048, 2048, 2048, 1024)
MULTIPLY_BLOCK = 2048
HEAD = 1536


def whole_in(space):
    return pl.BlockSpec(memory_space=space)


def slots_of(owner, upright=False):
    rows = owner.shape[1]
    across = jnp.broadcast_to(owner.astype(jnp.float32), (rows, rows))
    down = across.T
    first = lax.broadcasted_iota(jnp.int32, (rows, rows), 0)
    second = lax.broadcasted_iota(jnp.int32, (rows, rows), 1)
    if upright:
        earlier = jnp.where((across == down) & (second < first), 1, 0)
        return down[:, :1].astype(jnp.int32), jnp.sum(earlier, axis=1, keepdims=True)
    earlier = jnp.where((across == down) & (first < second), 1, 0)
    return jnp.sum(earlier, axis=0, keepdims=True)


def place_kernel(swap_ref, owner_ref, integrals_ref, out_ref, both_ref, placed_ref, pick_ref, sem):
    rows, (lines, width) = integrals_ref.shape[0], out_ref.shape
    starts = [sum(PLACE_BLOCKS[:i]) for i in range(len(PLACE_BLOCKS))]

    def fetch(i, half):
        start, block = starts[i], PLACE_BLOCKS[i]
        return pltpu.make_async_copy(
            integrals_ref.at[:, pl.ds(half * width + start, block)],
            both_ref.at[pl.ds(half * rows, rows), pl.ds(start, block)],
            sem.at[i, half],
        )

    fetches = [[fetch(i, half) for half in range(2)] for i in range(len(PLACE_BLOCKS))]
    for pair in fetches:
        for copy in pair:
            copy.start()

    owner = owner_ref[...]
    line = owner * BLOCK + slots_of(owner)
    number = lax.broadcasted_iota(jnp.int32, (lines, rows), 0)
    swap = swap_ref[0] * CAP
    pick_ref[:, :rows] = jnp.where(number == line + swap, 1.0, 0.0).astype(jnp.bfloat16)
    pick_ref[:, rows:] = jnp.where(number == line + (CAP - swap), 1.0, 0.0).astype(jnp.bfloat16)

    writes = []
    for i, pair in enumerate(fetches):
        for copy in pair:
            copy.wait()
        here = pl.ds(starts[i], PLACE_BLOCKS[i])
        placed_ref[:, here] = jnp.dot(
            pick_ref[...], both_ref[:, here], preferred_element_type=jnp.float32
        ).astype(jnp.bfloat16)
        writes.append(pltpu.make_async_copy(placed_ref.at[:, here], out_ref.at[:, here], sem.at[i, 2]))
        writes[-1].start()
    for write in writes:
        write.wait()


def place(swap, owner, integrals, peers):
    rows, cols = integrals.shape
    lines, width = peers * BLOCK, cols // 2
    return pl.pallas_call(
        place_kernel,
        in_specs=[whole_in(pltpu.SMEM), whole_in(pltpu.VMEM), whole_in(pl.ANY)],
        out_specs=whole_in(pl.ANY),
        out_shape=pltpu.HBM((lines, width), jnp.bfloat16),
        scratch_shapes=[
            pltpu.VMEM((2 * rows, width), jnp.bfloat16),
            pltpu.VMEM((lines, width), jnp.bfloat16),
            pltpu.VMEM((lines, 2 * rows), jnp.bfloat16),
            pltpu.SemaphoreType.DMA((len(PLACE_BLOCKS), 3)),
        ],
        compiler_params=pltpu.CompilerParams(vmem_limit_bytes=24 * 1024 * 1024),
        cost_estimate=pl.CostEstimate(
            flops=4 * lines * rows * width,
            bytes_accessed=2 * (2 * rows + lines) * width,
            transcendentals=0,
        ),
        name="place",
    )(swap, owner, pltpu.with_memory_space_constraint(integrals, pltpu.HBM))


def collect_kernel(
    amp_ref, owner_ref, mine_ref, left_ref, right_ref, top_ref, bottom_ref,
    out_ref, kept_ref, pick_ref, held_ref, sem,
):
    pairs = mine_ref.shape[0]
    count = out_ref.shape[0] // pairs
    shards = (
        (mine_ref, 0, 0),
        (left_ref, 1, 0),
        (right_ref, 3, 0),
        (top_ref, 2, 0),
        (bottom_ref, 2, pairs // 2),
    )
    fetches, writes = [], []
    for i, (ref, shift, skip) in enumerate(shards):
        at = (amp_ref[0] + count - shift) % count
        there = pl.ds(pl.multiple_of(at * pairs + skip, pairs // 2), ref.shape[0])
        fetches.append(pltpu.make_async_copy(ref, held_ref.at[there, :], sem.at[i, 0]))
        writes.append(
            pltpu.make_async_copy(held_ref.at[there, :], out_ref.at[there, :], sem.at[i, 1])
        )
    for copy in fetches:
        copy.start()
    owner, slot = slots_of(owner_ref[...], upright=True)
    lines = pick_ref.shape[1] // 2
    number = lax.broadcasted_iota(jnp.int32, (pick_ref.shape[0], lines), 1)
    here = jnp.where(number == owner * CAP + slot, 1.0, 0.0)
    pick_ref[:, :lines] = (here * 256.0).astype(jnp.bfloat16)
    pick_ref[:, lines:] = here.astype(jnp.bfloat16)
    for fetch, write in zip(fetches, writes):
        fetch.wait()
        write.start()
    kept, width = kept_ref.shape[1] // 2, out_ref.shape[1] // 2
    kept_ref[:, :kept] = held_ref[:, :kept]
    kept_ref[:, kept:] = held_ref[:, width : width + kept]
    for copy in writes:
        copy.wait()


def collect(amp, owner, shards, count, peers):
    pairs, cols = shards[0].shape
    kept = 2 * HEAD
    return pl.pallas_call(
        collect_kernel,
        in_specs=[whole_in(pltpu.SMEM), whole_in(pltpu.VMEM)] + [whole_in(pl.ANY)] * len(shards),
        out_specs=[whole_in(pl.ANY), whole_in(pltpu.VMEM), whole_in(pltpu.VMEM)],
        out_shape=[
            pltpu.HBM((count * pairs, cols), jnp.bfloat16),
            pltpu.VMEM((count * pairs, kept), jnp.bfloat16),
            jax.ShapeDtypeStruct((owner.shape[1], 2 * peers * CAP), jnp.bfloat16),
        ],
        scratch_shapes=[
            pltpu.VMEM((count * pairs, cols), jnp.bfloat16),
            pltpu.SemaphoreType.DMA((len(shards), 2)),
        ],
        compiler_params=pltpu.CompilerParams(vmem_limit_bytes=24 * 1024 * 1024),
        cost_estimate=pl.CostEstimate(
            flops=0, bytes_accessed=4 * count * pairs * cols, transcendentals=0
        ),
        name="collect",
    )(amp, owner, *[pltpu.with_memory_space_constraint(x, pltpu.HBM) for x in shards])


def exchange(x, group):
    lines = x.shape[0]
    return jnp.where(group == 0, pltpu.roll(x, lines - CAP, 0), pltpu.roll(x, CAP, 0))


def multiply_kernel(
    rows_ref, amps_ref, kept_ref, out_ref, near_ref, held_ref, low_ref, high_ref, sem
):
    lines, width = rows_ref.shape
    upper = lines // 2
    steps = (width - HEAD) // MULTIPLY_BLOCK
    tail = HEAD + steps * MULTIPLY_BLOCK

    def fetches(i, start, block, halves=2):
        at = [pl.ds(half * width + start, block) for half in range(2)]
        copies = [pltpu.make_async_copy(rows_ref.at[:, at[0]], near_ref.at[:, at[0]], sem.at[i, 0])]
        for half in range(halves):
            copies.append(
                pltpu.make_async_copy(
                    amps_ref.at[:, at[half]], held_ref.at[:, at[half]], sem.at[i, 1 + half]
                )
            )
        return copies

    def middle(i):
        start = pl.multiple_of(HEAD + i * MULTIPLY_BLOCK, 512)
        return fetches(1 + i, start, MULTIPLY_BLOCK), start

    def work(start, block, table_ref, half_width):
        group = lax.broadcasted_iota(jnp.int32, (upper, block), 0) // CAP % 2
        first, second = near_ref[:upper, pl.ds(start, block)], near_ref[upper:, pl.ds(start, block)]
        for half, total_ref in enumerate((low_ref, high_ref)):
            total_ref[...] += lax.dot_general(
                jnp.where(group == half, first, second),
                table_ref[:, pl.ds(half * half_width + start, block)],
                (((1,), (1,)), ((), ())),
                preferred_element_type=jnp.float32,
            )

    head = fetches(0, 0, HEAD, 0)[0]
    head.start()

    @pl.loop(0, steps)
    def _(i):
        for copy in middle(i)[0]:
            copy.start()

    rest = fetches(1 + steps, tail, width - tail)
    for copy in rest:
        copy.start()
    low_ref[...] = jnp.zeros_like(low_ref)
    high_ref[...] = jnp.zeros_like(high_ref)
    head.wait()
    work(0, HEAD, kept_ref, HEAD)

    @pl.loop(0, steps)
    def _(i):
        copies, start = middle(i)
        for copy in copies:
            copy.wait()
        work(start, MULTIPLY_BLOCK, held_ref, width)

    for copy in rest:
        copy.wait()
    work(tail, width - tail, held_ref, width)

    group = lax.broadcasted_iota(jnp.int32, low_ref.shape, 0) // CAP % 2
    value = low_ref[...] + exchange(high_ref[...], group)
    power = jnp.log2(jnp.maximum(jnp.max(jnp.abs(value), axis=1, keepdims=True), 2.0**-110))
    code = jnp.ceil(power * STEPS + 0.01).astype(jnp.int32)
    whole = jnp.round(value * (LARGEST / jnp.exp2(code.astype(jnp.float32) / STEPS)))
    whole = jnp.clip(whole, -LARGEST, LARGEST).astype(jnp.int32)
    whole = jnp.concatenate([whole, jnp.broadcast_to(code, (upper, LANES))], axis=1)
    blocks = whole.reshape(upper // BLOCK, 2, CAP, whole.shape[1])
    for j in range(2):
        first = j * (upper // BLOCK)
        out_ref[first : first + upper // BLOCK] = blocks[:, j].astype(jnp.int16)


def multiply(rows, amps, kept):
    lines, width = rows.shape
    pairs = amps.shape[0]
    return pl.pallas_call(
        multiply_kernel,
        in_specs=[whole_in(pl.ANY), whole_in(pl.ANY), whole_in(pltpu.VMEM)],
        out_specs=whole_in(pltpu.VMEM),
        out_shape=pltpu.VMEM((lines // BLOCK, CAP, pairs + LANES), jnp.int16),
        scratch_shapes=[
            pltpu.VMEM((lines, width), jnp.bfloat16),
            pltpu.VMEM((pairs, 2 * width), jnp.bfloat16),
            pltpu.VMEM((lines // 2, pairs), jnp.float32),
            pltpu.VMEM((lines // 2, pairs), jnp.float32),
            pltpu.SemaphoreType.DMA((2 + (width - HEAD) // MULTIPLY_BLOCK, 3)),
        ],
        compiler_params=pltpu.CompilerParams(vmem_limit_bytes=40 * 1024 * 1024),
        cost_estimate=pl.CostEstimate(
            flops=2 * lines * pairs * width,
            bytes_accessed=2 * (lines + 2 * pairs) * width,
            transcendentals=0,
        ),
        name="multiply",
    )(
        pltpu.with_memory_space_constraint(rows, pltpu.HBM),
        pltpu.with_memory_space_constraint(amps, pltpu.HBM),
        pltpu.with_memory_space_constraint(kept, pltpu.VMEM),
    )


def pick_kernel(matrix_ref, lines_ref, out_ref, pick_ref, parts_ref, held_ref, sem):
    lines, pairs = pick_ref.shape[1] // 2, out_ref.shape[1]
    fetch = pltpu.make_async_copy(matrix_ref, pick_ref, sem.at[0])
    fetch.start()
    whole = lines_ref[...].astype(jnp.int32).reshape(lines, lines_ref.shape[2])
    upper = whole >> 8
    parts_ref[:lines, :] = upper.astype(jnp.float32).astype(jnp.bfloat16)
    parts_ref[lines:, :] = (whole - (upper << 8)).astype(jnp.float32).astype(jnp.bfloat16)
    fetch.wait()

    def picked(first, count):
        return jnp.dot(
            pick_ref[...],
            parts_ref[:, first : first + count],
            preferred_element_type=jnp.float32,
        )

    unit = jnp.exp2(picked(pairs, LANES)[:, :1] / STEPS) / LARGEST
    writes = []
    for i in range(2):
        first, count = i * (pairs // 2), pairs // 2
        held_ref[:, first : first + count] = picked(first, count) * unit
        here = pl.ds(first, count)
        writes.append(pltpu.make_async_copy(held_ref.at[:, here], out_ref.at[:, here], sem.at[1 + i]))
        writes[-1].start()
    for write in writes:
        write.wait()


def pick(matrix, lines):
    rows, pairs = matrix.shape[0], lines.shape[2] - LANES
    return pl.pallas_call(
        pick_kernel,
        in_specs=[whole_in(pl.ANY), whole_in(pltpu.VMEM)],
        out_specs=whole_in(pl.ANY),
        out_shape=jax.ShapeDtypeStruct((rows, pairs), jnp.float32),
        scratch_shapes=[
            pltpu.VMEM(matrix.shape, jnp.bfloat16),
            pltpu.VMEM((matrix.shape[1], lines.shape[2]), jnp.bfloat16),
            pltpu.VMEM((rows, pairs), jnp.float32),
            pltpu.SemaphoreType.DMA((3,)),
        ],
        cost_estimate=pl.CostEstimate(
            flops=4 * rows * lines.size,
            bytes_accessed=2 * lines.size + 4 * rows * pairs,
            transcendentals=rows,
        ),
        name="pick",
    )(
        pltpu.with_memory_space_constraint(matrix, pltpu.HBM),
        pltpu.with_memory_space_constraint(lines, pltpu.VMEM),
    )


def body(integrals, row_owner, lambda_amps):
    peers, amps = lax.axis_size("kblk"), lax.axis_size("amp")
    amp = lax.axis_index("amp").astype(jnp.int32)
    swap = (lax.axis_index("kblk") >= peers // 2).astype(jnp.int32)
    mine = lambda_amps[0]
    middle = mine.shape[0] // 2
    ahead = [(i, (i + 1) % amps) for i in range(amps)]
    back = [(i, (i - 1) % amps) for i in range(amps)]
    left, right = lax.ppermute(mine, "amp", ahead), lax.ppermute(mine, "amp", back)
    top = lax.ppermute(left[:middle], "amp", ahead)
    bottom = lax.ppermute(right[middle:], "amp", back)
    owner = row_owner.reshape(1, -1)
    whole_lambda, kept, matrix = collect(
        amp[None], owner, (mine, left, right, top, bottom), amps, peers
    )

    placed = place(swap[None], owner, integrals, peers)
    width = placed.shape[1]
    arrived = lax.all_to_all(
        placed.reshape(peers, BLOCK, width), "kblk", split_axis=0, concat_axis=0, tiled=True
    )
    values = multiply(arrived.reshape(peers * BLOCK, width), whole_lambda, kept)
    returned = lax.all_to_all(values, "kblk", split_axis=0, concat_axis=0, tiled=True)
    return pick(matrix, returned)


def solution(mesh):
    placed = (P(("kblk", "amp"), None), P(("kblk", "amp"), None), P("kblk", "amp", None))
    return jax.shard_map(
        body, mesh=mesh, in_specs=placed, out_specs=P(("kblk", "amp"), None), check_vma=False
    )
```
